32 devices in a mesh: cases: 2 (over x), tx: 8 (over z, y), ty: 2 (over core).
Axes of the slice: x: 2, y: 2, z: 4, core: 2. Of those that a mesh axis runs over, the one named last changes fastest.
Arguments:
- tiles: bfloat16 [16, 2, 1024, 128], P(('cases', 'tx'), 'ty'), parts along dimension 0, may hold values from -6 to 6
- sources: int32 [16, 2, 1024, 8], P(('cases', 'tx'), 'ty'), parts along dimension 0, may hold values from 0 to 2047
- parents: int32 [16, 2, 1024], P(('cases', 'tx'), 'ty'), parts along dimension 0, may hold values from 0 to 1023, as said below
- restrict_w: bfloat16 [16, 2, 1024], P(('cases', 'tx'), 'ty'), parts along dimension 0, may hold values from 0.29882812 to 3
- coarse_state: bfloat16 [2048, 128], P(('cases', 'tx', 'ty')), parts along dimension 0, may hold values from -6 to 6
- edge_in: bfloat16 [2, 128, 128], replicated, may hold values from -0.5 to 0.5
- edge_bias: float32 [128], replicated, may hold values from -3 to 3
- edge_out: bfloat16 [128, 128], replicated, may hold values from -0.5 to 0.5
- node_in: bfloat16 [2, 128, 128], replicated, may hold values from -0.5 to 0.5
- node_bias: float32 [128], replicated, may hold values from -3 to 3
- node_out: bfloat16 [128, 128], replicated, may hold values from -0.5 to 0.5
- node_gain: float32 [128], replicated, may hold values from 0.1 to 1.9
- coarse_gain: float32 [128], replicated, may hold values from 0.1 to 1.9
- coarse_w: bfloat16 [2, 128, 128], replicated, may hold values from -0.5 to 0.5
- prolong_in: bfloat16 [2, 128, 128], replicated, may hold values from -0.5 to 0.5
- prolong_out: bfloat16 [128, 128], replicated, may hold values from -0.5 to 0.5
Outputs:
- fine_out: bfloat16 [16, 2, 1024, 128], P(('cases', 'tx'), 'ty'), parts along dimension 0
- coarse_out: bfloat16 [2048, 128], P(('cases', 'tx', 'ty')), parts along dimension 0
The draws below stay inside these ranges and needn't reach their ends.
There are 2 independent parts, one for each index of `cases`. The reference program is written for one: setup_inputs(seed, part) draws one part's arguments, and reference() takes and returns one part's arrays. A program takes and returns all parts, laid end to end along the dimension named above; an argument that names none is the same for every part. Nothing has to cross between parts.
Inputs may be any that keep to these rules, and one draw needn't show every extreme that they name: `parents`: tile (i, j) owns the coarse nodes (i * 2 + j) * 64 to (i * 2 + j + 1) * 64 - 1; the parent of each of its fine nodes lies in its own block or in the block of one of the tiles (i-1, j), (i+1, j), (i, j-1), (i, j+1) of the grid.
All inputs are finite; a program needn't handle non-finite values.
Results may differ from the reference program's by a relative error of at most 0.0047.
The reference program's roundings to bfloat16 on the way count: a program that leaves them out, or rounds other values in their place, can miss the bound.
Values may be sent and summed in bfloat16 or wider, within the bound.
No kernel may reach another device: no remote copies, remote signals or barrier semaphores. Data moves between devices by JAX's collectives and lax.ppermute only.
A program may use at most 64 MiB of HBM per device.

```python
import math
import jax
import jax.numpy as jnp
from jax import lax

F = 128
NODE_DEV = 1024
DEG = 8
CO_DEV = 64
BND = 256
TILES_X = 8
TILES_Y = 2
COARSE = 1024


def draw_parents(key, part):
    key = jax.random.fold_in(key, 11)
    key_pick, key_side, key_slot = jax.random.split(key, 3)
    shape = (TILES_X, TILES_Y, NODE_DEV)
    pick = jax.random.randint(key_pick, shape, 0, 10)
    side = jax.random.randint(key_side, shape, 0, 4)
    slot = jax.random.randint(key_slot, shape, 0, CO_DEV)
    row_idx = jnp.arange(TILES_X, dtype=jnp.int32)[:, None, None]
    col_idx = jnp.arange(TILES_Y, dtype=jnp.int32)[None, :, None]
    away = pick >= 8
    step_x = jnp.where(side == 0, -1, jnp.where(side == 1, 1, 0))
    step_y = jnp.where(side == 2, -1, jnp.where(side == 3, 1, 0))
    near_x = row_idx + jnp.where(away, step_x, 0)
    near_y = col_idx + jnp.where(away, step_y, 0)
    inside = (near_x >= 0) & (near_x < TILES_X) & (near_y >= 0) & (near_y < TILES_Y)
    near_x = jnp.where(inside, near_x, row_idx)
    near_y = jnp.where(inside, near_y, col_idx)
    return ((near_x * TILES_Y + near_y) * CO_DEV + slot).astype(jnp.int32)


def place_ends(entries, own_key, low, largest):
    shape = entries.shape
    place = [jax.random.randint(jax.random.fold_in(own_key, axis), (), 0, shape[axis]) for axis in range(len(shape))]
    entries = entries.at[tuple(place)].set(low)
    longest = shape.index(max(shape))
    place[longest] = (place[longest] + 1) % shape[longest]
    return entries.at[tuple(place)].set(largest)


def block_levels(key, dims, cuts, smallest, largest):
    level = 1.0
    for axis_at, shards_of in cuts:
        steps = jax.random.uniform(jax.random.fold_in(jax.random.fold_in(key, 6), axis_at), (shards_of,), jnp.float32, smallest / len(cuts), largest / len(cuts))
        level = level * jnp.repeat(jnp.exp(steps), dims[axis_at] // shards_of).reshape((-1,) + (1,) * (len(dims) - 1 - axis_at))
    return level


def normal_values(rng, dims, scale, reach, cuts=(), held_as=jnp.bfloat16):
    values = scale * jax.random.normal(rng, dims, jnp.float32)
    if cuts:
        values = values * block_levels(rng, dims, cuts, -0.22, 0.18)
    return jnp.clip(values, -reach, reach).astype(held_as)


def setup_inputs(seed: int = 0, part: int = 0) -> dict:
    arg_keys = jax.random.split(jax.random.key(seed), 17)
    part_splits = jax.random.split(jax.random.fold_in(arg_keys[16], part), 17)
    return {
        "tiles": normal_values(part_splits[0], (TILES_X, TILES_Y, NODE_DEV, F), 1.0, 6.0, ((0, 8), (1, 2))),
        "sources": place_ends(jax.random.randint(part_splits[1], (TILES_X, TILES_Y, NODE_DEV, DEG), 0, NODE_DEV + 4 * BND), jax.random.fold_in(part_splits[1], 1), 0, (NODE_DEV + 4 * BND) - 1).astype(jnp.int32),
        "parents": draw_parents(jax.random.fold_in(jax.random.fold_in(arg_keys[16], part), 71), part),
        "restrict_w": jnp.clip(jnp.exp(math.log(3.0) - 2.306499 * jax.random.uniform(part_splits[3], (TILES_X, TILES_Y, NODE_DEV), jnp.float32) ** block_levels(part_splits[3], (TILES_X, TILES_Y, NODE_DEV), ((0, 8), (1, 2)), -0.2, 0.2)), 0.29882812, 3.0).astype(jnp.bfloat16),
        "coarse_state": normal_values(part_splits[4], (COARSE, F), 1.0, 6.0, ((0, 16),)),
        "edge_in": normal_values(arg_keys[5], (2, F, F), F ** -0.5, 0.5),
        "edge_bias": normal_values(arg_keys[6], (F,), 0.5, 3.0, (), jnp.float32),
        "edge_out": normal_values(arg_keys[7], (F, F), F ** -0.5, 0.5),
        "node_in": normal_values(arg_keys[8], (2, F, F), F ** -0.5, 0.5),
        "node_bias": normal_values(arg_keys[9], (F,), 0.5, 3.0, (), jnp.float32),
        "node_out": normal_values(arg_keys[10], (F, F), F ** -0.5, 0.5),
        "node_gain": jnp.clip(1.0 + 0.18 * jax.random.normal(arg_keys[11], (F,), jnp.float32), 0.1, 1.9),
        "coarse_gain": jnp.clip(1.0 + 0.18 * jax.random.normal(arg_keys[12], (F,), jnp.float32), 0.1, 1.9),
        "coarse_w": normal_values(arg_keys[13], (2, F, F), F ** -0.5, 0.5),
        "prolong_in": normal_values(arg_keys[14], (2, F, F), F ** -0.5, 0.5),
        "prolong_out": normal_values(arg_keys[15], (F, F), F ** -0.5, 0.5),
    }


def layer_norm(values, gain):
    center = values - lax.optimization_barrier(jnp.mean(values, axis=-1, keepdims=True))
    spread = lax.optimization_barrier(jnp.mean(center * center, axis=-1, keepdims=True))
    return center * lax.rsqrt(spread + 1e-05) * gain

def tile_update(latents, beside_all, sources, edge_in, edge_bias, edge_out, node_in, node_bias, node_out, node_gain):
    extended = jnp.concatenate([latents, beside_all], axis=0)
    dst_proj = jnp.dot(latents, edge_in[0], preferred_element_type=jnp.float32)
    src_proj = jnp.dot(extended, edge_in[1], preferred_element_type=jnp.float32)
    picked = jnp.take(src_proj, sources.reshape(-1), axis=0).reshape(sources.shape[0], sources.shape[1], -1)
    edge_hidden = jax.nn.silu(dst_proj[:, None, :] + picked + edge_bias).astype(jnp.bfloat16)
    messages = jnp.dot(edge_hidden.reshape(-1, edge_hidden.shape[2]), edge_out, preferred_element_type=jnp.float32)
    aggregate = lax.optimization_barrier(jnp.sum(messages.reshape(sources.shape[0], sources.shape[1], -1), axis=1)).astype(jnp.bfloat16)
    node_pre = jnp.dot(latents, node_in[0], preferred_element_type=jnp.float32) + jnp.dot(aggregate, node_in[1], preferred_element_type=jnp.float32) + node_bias
    node_hidden = jax.nn.silu(node_pre).astype(jnp.bfloat16)
    update = jnp.dot(node_hidden, node_out, preferred_element_type=jnp.float32)
    return (latents.astype(jnp.float32) + layer_norm(update, node_gain)).astype(jnp.bfloat16)

def coarse_update(coarse_in, coarse_gain, coarse_w):
    normed = layer_norm(coarse_in, coarse_gain).astype(jnp.bfloat16)
    hidden = jax.nn.silu(jnp.dot(normed, coarse_w[0], preferred_element_type=jnp.float32)).astype(jnp.bfloat16)
    return (coarse_in + jnp.dot(hidden, coarse_w[1], preferred_element_type=jnp.float32)).astype(jnp.bfloat16)

def prolong(fine_mid, lifted, prolong_in, prolong_out):
    pre = jnp.dot(fine_mid, prolong_in[0], preferred_element_type=jnp.float32) + jnp.dot(lifted, prolong_in[1], preferred_element_type=jnp.float32)
    hidden = jax.nn.silu(pre).astype(jnp.bfloat16)
    return (fine_mid.astype(jnp.float32) + jnp.dot(hidden, prolong_out, preferred_element_type=jnp.float32)).astype(jnp.bfloat16)

def reference(tiles, sources, parents, restrict_w, coarse_state, edge_in, edge_bias, edge_out, node_in, node_bias, node_out, node_gain, coarse_gain, coarse_w, prolong_in, prolong_out):
    rim = tiles[:, :, :BND]
    padded = jnp.pad(rim, ((1, 1), (1, 1), (0, 0), (0, 0)))
    beside_all = jnp.concatenate([padded[:-2, 1:-1], padded[2:, 1:-1], padded[1:-1, :-2], padded[1:-1, 2:]], axis=2)
    count = TILES_X * TILES_Y
    flat_tiles = tiles.reshape(count, NODE_DEV, F)
    flat_around = beside_all.reshape(count, 4 * BND, F)
    flat_sources = sources.reshape(count, NODE_DEV, DEG)

    def one_tile(items):
        return tile_update(items[0], items[1], items[2], edge_in, edge_bias, edge_out, node_in, node_bias, node_out, node_gain)
    fine_mid = lax.map(one_tile, (flat_tiles, flat_around, flat_sources))
    weighted = (fine_mid.astype(jnp.float32) * restrict_w.reshape(count, NODE_DEV, 1).astype(jnp.float32)).astype(jnp.bfloat16)
    pooled = jax.ops.segment_sum(weighted.reshape(-1, F).astype(jnp.float32), parents.reshape(-1), num_segments=COARSE)
    coarse_in = coarse_state.astype(jnp.float32) + pooled
    coarse_out = coarse_update(coarse_in, coarse_gain, coarse_w)
    lifted = jnp.take(coarse_out, parents.reshape(count, NODE_DEV), axis=0)

    def one_prolong(items):
        return prolong(items[0], items[1], prolong_in, prolong_out)
    fine_out = lax.map(one_prolong, (fine_mid, lifted))
    return (fine_out.reshape(TILES_X, TILES_Y, NODE_DEV, F), coarse_out)
```

```python
import functools

import jax
import jax.numpy as jnp
from jax import lax
from jax.experimental import pallas as pl
from jax.experimental.pallas import tpu as pltpu
from jax.sharding import PartitionSpec as P

F32 = jnp.float32
BF16 = jnp.bfloat16
I32 = jnp.int32
VMEM_LIMIT = 32 * 1024 * 1024
BLOCK = 128
GROUP = 4


def mm(a, b):
    return jnp.dot(a, b, preferred_element_type=F32)


def silu(x):
    half = 0.5 * x
    return half + half * jnp.tanh(half)


def normalise(values, gain):
    center = values - jnp.mean(values, axis=-1, keepdims=True)
    spread = jnp.mean(center * center, axis=-1, keepdims=True)
    return center * lax.rsqrt(spread + 1e-05) * gain


def split(values):
    high = values.astype(BF16)
    low = (values - high.astype(F32)).astype(BF16)
    return jnp.concatenate([high, low], axis=1)


def quotient(x, d):
    return lax.shift_right_logical(x, d.bit_length() - 1) if d & (d - 1) == 0 else x // d


def place(n):
    i, j = lax.axis_index("tx"), lax.axis_index("ty")
    return i, j, lax.rem(i, 2) == 0


def owners(n):
    i, j, even = place(n)
    mine = i * 2 + j
    return mine, jnp.where(even, mine + 2, mine - 2), jnp.where(even, mine - 2, mine + 2), mine + 1 - 2 * j


def spread(cols, lane, rows):
    return jnp.broadcast_to(cols[:, lane : lane + 1], (rows, 128))


def one_hot(where, first, count):
    parts = []
    for at in range(first, first + count, 128):
        lanes = (lax.broadcasted_iota(I32, where.shape, 1) + at).astype(F32).astype(BF16)
        parts.append(jnp.where(where == lanes, jnp.ones((), BF16), jnp.zeros((), BF16)))
    return jnp.concatenate(parts, axis=1)


def gathered(cols, table, degree, block):
    rim = table.shape[0] // 2
    pairs = []
    for k in range(0, degree, GROUP):
        ones = jnp.concatenate([one_hot(spread(cols, k + g, block), -rim, 2 * rim) for g in range(GROUP)], axis=0)
        got = mm(ones, table).astype(BF16)
        for g in range(GROUP):
            part = got[g * block : (g + 1) * block]
            pairs.append((part[:, :128], part[:, 128:], spread(cols, degree + k + g, block)))
    return pairs


def local_kernel(tiles, sources, cols, near):
    nodes, width = tiles.shape
    degree = sources.shape[0]
    rim = nodes // 4
    index = sources[...]
    rows = jnp.concatenate([((index & (2 * rim - 1)) - rim).astype(F32), quotient(index, 2 * rim).astype(F32)], axis=0)
    cols[...] = rows.T.astype(BF16)
    table = jnp.concatenate([tiles[: 2 * rim, :], tiles[2 * rim :, :]], axis=1)

    def step(at, _):
        first = pl.multiple_of(at * BLOCK, BLOCK)
        here = pl.ds(first, BLOCK)
        for k, (low, high, quarter) in enumerate(gathered(cols[here, :], table, degree, BLOCK)):
            near[k, here, :] = jnp.where(quarter == jnp.ones((), BF16), high, low)
        return 0

    lax.fori_loop(0, nodes // BLOCK, step, 0)


def node_kernel(
    n, tiles, around_a, around_b, around_s, cols, near, parents, weights,
    edge_in, edge_bias, edge_out, node_in, node_bias, node_out, node_gain,
    fine_mid, own, to_a, to_b, to_s, slots, total, weighted,
):
    nodes, width = tiles.shape
    degree = near.shape[0]
    co_rows = own.shape[0]
    i, j, even = place(n)
    none = jnp.zeros(around_a.shape, BF16)
    got_a, got_b, got_s = around_a[...], around_b[...], around_s[...]
    before = jnp.where(i > 0, jnp.where(even, got_b, got_a), none)
    after = jnp.where(i < n - 1, jnp.where(even, got_a, got_b), none)
    left, right = jnp.where(j > 0, got_s, none), jnp.where(j < 1, got_s, none)
    table = jnp.concatenate([jnp.concatenate([before, left], axis=1), jnp.concatenate([after, right], axis=1)], axis=0)
    project = edge_in[1]
    empty = jnp.zeros_like(project)
    project = jnp.concatenate(
        [jnp.concatenate([project, empty], axis=1), jnp.concatenate([empty, project], axis=1)], axis=0
    )

    def step(at, _):
        first = pl.multiple_of(at * BLOCK, BLOCK)
        here = pl.ds(first, BLOCK)
        dst_part = mm(tiles[here, :], edge_in[0]) + edge_bias[...]
        picked = []
        for k, (low, high, quarter) in enumerate(gathered(cols[here, :], table, degree, BLOCK)):
            far = jnp.where(quarter == jnp.full((), 3, BF16), high, low)
            picked.append(jnp.where(quarter < jnp.full((), 2, BF16), near[k, here, :], far))
        picked = jnp.concatenate(
            [jnp.concatenate([picked[k], picked[k + 1]], axis=1) for k in range(0, degree, 2)], axis=0
        )
        src = mm(picked, project)
        sums = jnp.zeros((BLOCK, width), F32)
        for k in range(degree):
            part = src[k // 2 * BLOCK : (k // 2 + 1) * BLOCK, k % 2 * width : (k % 2 + 1) * width]
            sums = sums + silu(dst_part + part).astype(BF16).astype(F32)
        total[here, :] = sums
        return 0

    lax.fori_loop(0, nodes // BLOCK, step, 0)
    node_weights = jnp.concatenate([node_in[0], node_in[1]], axis=0)
    out_twice = jnp.concatenate([edge_out[...], edge_out[...]], axis=0)
    ids = parents[...]
    block_of = quotient(ids, co_rows)
    slot = ids - block_of * co_rows
    for at, owner in enumerate(owners(n)):
        slot = jnp.where(block_of == owner, slot + at * co_rows, slot)
    slot = slot.astype(F32)
    scale = jnp.concatenate([slot, weights[...].astype(F32), jnp.zeros((6, nodes), F32)], axis=0).T
    slots[...] = scale.astype(BF16)
    for first in range(0, nodes, 256):
        here = pl.ds(first, 256)
        aggregate = mm(split(total[here, :]), out_twice).astype(BF16)
        both = jnp.concatenate([tiles[here, :], aggregate], axis=1)
        hidden = silu(mm(both, node_weights) + node_bias[...]).astype(BF16)
        update = normalise(mm(hidden, node_out[...]), node_gain[...])
        mid = (tiles[here, :].astype(F32) + update).astype(BF16)
        fine_mid[here, :] = mid
        weighted[here, :] = (mid.astype(F32) * scale[first : first + 256, 1:2]).astype(BF16)
    row = lax.broadcasted_iota(I32, (4 * co_rows, nodes), 0).astype(F32).astype(BF16)
    ones = jnp.where(row == slot.astype(BF16), jnp.ones((), BF16), jnp.zeros((), BF16))
    pooled = mm(ones, weighted[...])
    for at, ref in enumerate((own, to_a, to_b, to_s)):
        ref[...] = pooled[at * co_rows : (at + 1) * co_rows]


def coarse_kernel(state, own, from_a, from_b, from_s, coarse_gain, coarse_w, out):
    total = state[...].astype(F32) + own[...] + from_a[...] + from_b[...] + from_s[...]
    normed = normalise(total, coarse_gain[...]).astype(BF16)
    hidden = silu(mm(normed, coarse_w[0])).astype(BF16)
    out[...] = (total + mm(hidden, coarse_w[1])).astype(BF16)


def prolong_kernel(fine_mid, slots, own, from_a, from_b, from_s, prolong_in, prolong_out, out):
    nodes, width = fine_mid.shape
    co_rows = own.shape[0]
    coarse = jnp.concatenate([own[...], from_a[...], from_b[...], from_s[...]], axis=0)
    weights = jnp.concatenate([prolong_in[0], prolong_in[1]], axis=0)
    block = 256
    for first in range(0, nodes, block):
        here = pl.ds(first, block)
        ones = one_hot(spread(slots[here, :], 0, block), 0, 4 * co_rows)
        lifted = mm(ones, coarse).astype(BF16)
        mid = fine_mid[here, :]
        hidden = silu(mm(jnp.concatenate([mid, lifted], axis=1), weights)).astype(BF16)
        out[here, :] = (mid.astype(F32) + mm(hidden, prolong_out[...])).astype(BF16)


def call(kernel, outs, *args, flops=0, scratch=()):
    return pl.pallas_call(
        kernel,
        out_shape=outs,
        in_specs=[pl.BlockSpec(memory_space=pltpu.VMEM)] * len(args),
        out_specs=[pl.BlockSpec(memory_space=pltpu.VMEM)] * len(outs),
        scratch_shapes=scratch,
        compiler_params=pltpu.CompilerParams(vmem_limit_bytes=VMEM_LIMIT),
        cost_estimate=pl.CostEstimate(flops=flops, bytes_accessed=flops // 1000, transcendentals=0),
    )(*args)


def exchange(n, to_a, to_b, to_s):
    pairs_a = [(i, i ^ 1) for i in range(n)]
    pairs_b = []
    for i in range(n):
        for j in range(2):
            other = (((i - 1) ^ 1) + 1, j) if 0 < i < n - 1 else (i, 1 - j)
            pairs_b.append((i * 2 + j, other[0] * 2 + other[1]))
    return (
        lax.ppermute(to_a, "tx", pairs_a),
        lax.ppermute(to_b, ("tx", "ty"), pairs_b),
        lax.ppermute(to_s, "ty", [(0, 1), (1, 0)]),
    )


def body(
    tiles,
    sources,
    parents,
    restrict_w,
    coarse_state,
    edge_in,
    edge_bias,
    edge_out,
    node_in,
    node_bias,
    node_out,
    node_gain,
    coarse_gain,
    coarse_w,
    prolong_in,
    prolong_out,
):
    nodes, width = tiles.shape[2:]
    n = lax.axis_size("tx")
    co_rows = coarse_state.shape[0]
    degree = sources.shape[3]
    shape = jax.ShapeDtypeStruct

    latents = tiles[0, 0]
    boundary = latents[: nodes // 4]
    around = exchange(n, boundary, boundary, boundary)
    cols, near = call(
        local_kernel,
        [shape((nodes, 2 * degree), BF16), shape((degree, nodes, width), BF16)],
        latents, jnp.swapaxes(sources[0, 0], 0, 1),
        flops=4 * 2**30,
    )
    fine_mid, own, to_a, to_b, to_s, slots = call(
        functools.partial(node_kernel, n),
        [shape((nodes, width), BF16)] + [shape((co_rows, width), F32)] * 4 + [shape((nodes, 8), BF16)],
        latents, *around, cols, near, parents[0], restrict_w[0],
        edge_in, edge_bias[None], edge_out, node_in, node_bias[None], node_out, node_gain[None],
        flops=6 * 2**30,
        scratch=[pltpu.VMEM((nodes, width), F32), pltpu.VMEM((nodes, width), BF16)],
    )
    got = exchange(n, to_a, to_b, to_s)
    (coarse_out,) = call(
        coarse_kernel,
        [shape((co_rows, width), BF16)],
        coarse_state, own, *got, coarse_gain[None], coarse_w,
        flops=2**29,
    )
    beside = exchange(n, coarse_out, coarse_out, coarse_out)
    (fine_out,) = call(
        prolong_kernel,
        [shape((nodes, width), BF16)],
        fine_mid, slots, coarse_out, *beside, prolong_in, prolong_out,
        flops=2**30,
    )
    return (fine_out[None, None], coarse_out)


def solution(mesh):
    tile = P(("cases", "tx"), "ty", None, None)
    row = P(("cases", "tx"), "ty", None)
    coarse = P(("cases", "tx", "ty"), None)
    return jax.shard_map(
        body,
        mesh=mesh,
        in_specs=(tile, tile, row, row, coarse) + (P(),) * 11,
        out_specs=(tile, coarse),
        check_vma=False,
    )
```

```python
import functools

import jax
import jax.numpy as jnp
from jax import lax
from jax.experimental import pallas as pl
from jax.experimental.pallas import tpu as pltpu
from jax.sharding import PartitionSpec as P

F32 = jnp.float32
BF16 = jnp.bfloat16
I32 = jnp.int32
VMEM_LIMIT = 32 * 1024 * 1024
BLOCK = 128
GROUP = 2
UNROLL = 8


def mm(a, b):
    return jnp.dot(a, b, preferred_element_type=F32)


def silu(x):
    half = 0.5 * x
    return half + half * jnp.tanh(half)


def normalise(values, gain):
    center = values - jnp.mean(values, axis=-1, keepdims=True)
    spread = jnp.mean(center * center, axis=-1, keepdims=True)
    return center * lax.rsqrt(spread + 1e-05) * gain


def split(values):
    high = values.astype(BF16)
    low = (values - high.astype(F32)).astype(BF16)
    return jnp.concatenate([high, low], axis=1)


def quotient(x, d):
    return lax.shift_right_logical(x, d.bit_length() - 1) if d & (d - 1) == 0 else x // d


def place(n):
    i, j = lax.axis_index("tx"), lax.axis_index("ty")
    return i, j, lax.rem(i, 2) == 0


def owners(n):
    i, j, even = place(n)
    mine = i * 2 + j
    return mine, jnp.where(even, mine + 2, mine - 2), jnp.where(even, mine - 2, mine + 2), mine + 1 - 2 * j


def spread(cols, lane, rows):
    return jnp.broadcast_to(cols[:, lane : lane + 1], (rows, 128)).astype(BF16)


def one_hot(where, first, count):
    parts = []
    for at in range(first, first + count, 128):
        lanes = (lax.broadcasted_iota(I32, where.shape, 1) + at).astype(F32).astype(BF16)
        parts.append(jnp.where(where == lanes, jnp.ones((), BF16), jnp.zeros((), BF16)))
    return jnp.concatenate(parts, axis=1)


def gathered(cols, table, degree, block):
    rim = table.shape[0] // 2
    pairs = []
    for k in range(0, degree, GROUP):
        ones = jnp.concatenate([one_hot(spread(cols, k + g, block), -rim, 2 * rim) for g in range(GROUP)], axis=0)
        got = mm(ones, table).astype(BF16)
        for g in range(GROUP):
            part = got[g * block : (g + 1) * block]
            pairs.append((part[:, :128], part[:, 128:], spread(cols, degree + k + g, block)))
    return pairs


def boundary_kernel(tiles, boundary):
    boundary[...] = tiles[: boundary.shape[0], :]


def local_kernel(
    n, co_rows, tiles, sources, parents, weights, edge_in, edge_bias, cols, near, dst, scale, pool, lift
):
    nodes, width = tiles.shape
    degree = near.shape[0]
    rim = nodes // 4
    index = sources[...]
    ids = parents[...]
    block_of = quotient(ids, co_rows)
    slot = ids - block_of * co_rows
    for at, owner in enumerate(owners(n)):
        slot = jnp.where(block_of == owner, slot + at * co_rows, slot)
    slot = slot.astype(F32)
    rows = [
        ((index & (2 * rim - 1)) - rim).astype(F32),
        quotient(index, 2 * rim).astype(F32),
        slot,
        weights[...].astype(F32),
        jnp.zeros((6, nodes), F32),
    ]
    turned = jnp.concatenate(rows, axis=0).T
    cols[...] = turned
    scale[...] = turned[:, 2 * degree + 1 : 2 * degree + 2] * jnp.ones((1, width), F32)
    dst[...] = mm(tiles[...], edge_in[0]) + edge_bias[...]
    row = lax.broadcasted_iota(I32, pool.shape, 0).astype(F32).astype(BF16)
    pool[...] = jnp.where(row == slot.astype(BF16), jnp.ones((), BF16), jnp.zeros((), BF16))
    lift[...] = one_hot(spread(cols[...], 2 * degree, nodes), 0, 4 * co_rows)
    table = jnp.concatenate([tiles[: 2 * rim, :], tiles[2 * rim :, :]], axis=1)

    def step(at, _):
        first = pl.multiple_of(at * BLOCK, BLOCK)
        here = pl.ds(first, BLOCK)
        for k, (low, high, quarter) in enumerate(gathered(cols[here, :], table, degree, BLOCK)):
            near[k, here, :] = jnp.where(quarter == jnp.ones((), BF16), high, low)
        return 0

    lax.fori_loop(0, nodes // BLOCK, step, 0, unroll=UNROLL)


def node_kernel(
    n, tiles, around_a, around_b, around_s, cols, near, dst, scale, pool,
    edge_in, edge_out, node_in, node_bias, node_out, node_gain,
    fine_mid, own, to_a, to_b, to_s, total, weighted,
):
    nodes, width = tiles.shape
    degree = near.shape[0]
    co_rows = own.shape[0]
    i, j, even = place(n)
    none = jnp.zeros(around_a.shape, BF16)
    got_a, got_b, got_s = around_a[...], around_b[...], around_s[...]
    before = jnp.where(i > 0, jnp.where(even, got_b, got_a), none)
    after = jnp.where(i < n - 1, jnp.where(even, got_a, got_b), none)
    left, right = jnp.where(j > 0, got_s, none), jnp.where(j < 1, got_s, none)
    table = jnp.concatenate([jnp.concatenate([before, left], axis=1), jnp.concatenate([after, right], axis=1)], axis=0)
    project = edge_in[1]
    empty = jnp.zeros_like(project)
    project = jnp.concatenate(
        [jnp.concatenate([project, empty], axis=1), jnp.concatenate([empty, project], axis=1)], axis=0
    )

    def step(at, _):
        first = pl.multiple_of(at * BLOCK, BLOCK)
        here = pl.ds(first, BLOCK)
        dst_part = dst[here, :]
        sums = jnp.zeros((BLOCK, width), F32)
        picked = []
        for k, (low, high, quarter) in enumerate(gathered(cols[here, :], table, degree, BLOCK)):
            far = jnp.where(quarter == jnp.full((), 3, BF16), high, low)
            picked.append(jnp.where(quarter < jnp.full((), 2, BF16), near[k, here, :], far))
        for k in range(0, degree, 2):
            got = mm(jnp.concatenate([picked[k], picked[k + 1]], axis=1), project)
            for part in (got[:, :width], got[:, width:]):
                sums = sums + silu(dst_part + part).astype(BF16).astype(F32)
        total[here, :] = sums
        return 0

    lax.fori_loop(0, nodes // BLOCK, step, 0, unroll=UNROLL)
    node_weights = jnp.concatenate([node_in[0], node_in[1]], axis=0)
    out_twice = jnp.concatenate([edge_out[...], edge_out[...]], axis=0)
    for first in range(0, nodes, 256):
        here = pl.ds(first, 256)
        aggregate = mm(split(total[here, :]), out_twice).astype(BF16)
        both = jnp.concatenate([tiles[here, :], aggregate], axis=1)
        hidden = silu(mm(both, node_weights) + node_bias[...]).astype(BF16)
        update = normalise(mm(hidden, node_out[...]), node_gain[...])
        mid = (tiles[here, :].astype(F32) + update).astype(BF16)
        fine_mid[here, :] = mid
        weighted[here, :] = (mid.astype(F32) * scale[here, :]).astype(BF16)
    pooled = mm(pool[...], weighted[...])
    for at, ref in enumerate((own, to_a, to_b, to_s)):
        ref[...] = pooled[at * co_rows : (at + 1) * co_rows]


def base_kernel(fine_mid, prolong_in, base):
    base[...] = mm(fine_mid[...], prolong_in[0])


def coarse_kernel(state, own, from_a, from_b, from_s, coarse_gain, coarse_w, out):
    total = state[...].astype(F32) + own[...] + from_a[...] + from_b[...] + from_s[...]
    normed = normalise(total, coarse_gain[...]).astype(BF16)
    hidden = silu(mm(normed, coarse_w[0])).astype(BF16)
    out[...] = (total + mm(hidden, coarse_w[1])).astype(BF16)


def prolong_kernel(fine_mid, base, lift, own, from_a, from_b, from_s, prolong_in, prolong_out, out, coarse_out):
    coarse_out[...] = own[...]
    nodes, width = fine_mid.shape
    coarse = jnp.concatenate([own[...], from_a[...], from_b[...], from_s[...]], axis=0)
    terms = split(mm(coarse, prolong_in[1]))
    block = 256
    for first in range(0, nodes, block):
        here = pl.ds(first, block)
        lifted = mm(lift[here, :], terms)
        hidden = silu(base[here, :] + (lifted[:, :width] + lifted[:, width:])).astype(BF16)
        out[here, :] = (fine_mid[here, :].astype(F32) + mm(hidden, prolong_out[...])).astype(BF16)


def call(kernel, outs, *args, flops=0, scratch=()):
    return pl.pallas_call(
        kernel,
        out_shape=outs,
        in_specs=[pl.BlockSpec(memory_space=pltpu.VMEM)] * len(args),
        out_specs=[pl.BlockSpec(memory_space=pltpu.VMEM)] * len(outs),
        scratch_shapes=scratch,
        compiler_params=pltpu.CompilerParams(vmem_limit_bytes=VMEM_LIMIT),
        cost_estimate=pl.CostEstimate(flops=flops, bytes_accessed=flops // 1000, transcendentals=0),
    )(*args)


def exchange(n, to_a, to_b, to_s):
    pairs_a = [(i, i ^ 1) for i in range(n)]
    pairs_b = []
    for i in range(n):
        for j in range(2):
            other = (((i - 1) ^ 1) + 1, j) if 0 < i < n - 1 else (i, 1 - j)
            pairs_b.append((i * 2 + j, other[0] * 2 + other[1]))
    return (
        lax.ppermute(to_a, "tx", pairs_a),
        lax.ppermute(to_b, ("tx", "ty"), pairs_b),
        lax.ppermute(to_s, "ty", [(0, 1), (1, 0)]),
    )


def body(
    tiles,
    sources,
    parents,
    restrict_w,
    coarse_state,
    edge_in,
    edge_bias,
    edge_out,
    node_in,
    node_bias,
    node_out,
    node_gain,
    coarse_gain,
    coarse_w,
    prolong_in,
    prolong_out,
):
    nodes, width = tiles.shape[2:]
    n = lax.axis_size("tx")
    co_rows = coarse_state.shape[0]
    degree = sources.shape[3]
    shape = jax.ShapeDtypeStruct

    latents = tiles[0, 0]
    (boundary,) = call(boundary_kernel, [shape((nodes // 4, width), BF16)], latents, flops=2**33)
    around = exchange(n, boundary, boundary, boundary)
    cols, near, dst, scale, pool, lift = call(
        functools.partial(local_kernel, n, co_rows),
        [
            shape((nodes, 24), F32),
            shape((degree, nodes, width), BF16),
            shape((nodes, width), F32),
            shape((nodes, width), F32),
            shape((4 * co_rows, nodes), BF16),
            shape((nodes, 4 * co_rows), BF16),
        ],
        latents, jnp.swapaxes(sources[0, 0], 0, 1), parents[0], restrict_w[0], edge_in, edge_bias[None],
        flops=2**34,
    )
    fine_mid, own, to_a, to_b, to_s = call(
        functools.partial(node_kernel, n),
        [shape((nodes, width), BF16)] + [shape((co_rows, width), F32)] * 4,
        latents, *around, cols, near, dst, scale, pool,
        edge_in, edge_out, node_in, node_bias[None], node_out, node_gain[None],
        flops=2**34,
        scratch=[pltpu.VMEM((nodes, width), F32), pltpu.VMEM((nodes, width), BF16)],
    )
    got = exchange(n, to_a, to_b, to_s)
    (coarse_out,) = call(
        coarse_kernel,
        [shape((co_rows, width), BF16)],
        coarse_state, own, *got, coarse_gain[None], coarse_w,
        flops=2**32,
    )
    beside = exchange(n, coarse_out, coarse_out, coarse_out)
    (base,) = call(base_kernel, [shape((nodes, width), F32)], fine_mid, prolong_in, flops=2**29)
    fine_out, coarse_out = call(
        prolong_kernel,
        [shape((nodes, width), BF16), shape((co_rows, width), BF16)],
        fine_mid, base, lift, coarse_out, *beside, prolong_in, prolong_out,
        flops=2**32,
    )
    return (fine_out[None, None], coarse_out)


def solution(mesh):
    tile = P(("cases", "tx"), "ty", None, None)
    row = P(("cases", "tx"), "ty", None)
    coarse = P(("cases", "tx", "ty"), None)
    return jax.shard_map(
        body,
        mesh=mesh,
        in_specs=(tile, tile, row, row, coarse) + (P(),) * 11,
        out_specs=(tile, coarse),
        check_vma=False,
    )
```

```python
import functools

import jax
import jax.numpy as jnp
from jax import lax
from jax.experimental import pallas as pl
from jax.experimental.pallas import tpu as pltpu
from jax.sharding import PartitionSpec as P

F32 = jnp.float32
BF16 = jnp.bfloat16
I32 = jnp.int32
VMEM_LIMIT = 32 * 1024 * 1024
BLOCK = 128
GROUP = 2
UNROLL = 8
CHUNK = 1024
PARTS = 4


def mm(a, b):
    return jnp.dot(a, b, preferred_element_type=F32)


def silu(x):
    half = 0.5 * x
    return half + half * jnp.tanh(half)


def normalise(values, gain):
    center = values - jnp.mean(values, axis=-1, keepdims=True)
    spread = jnp.mean(center * center, axis=-1, keepdims=True)
    return center * lax.rsqrt(spread + 1e-05) * gain


def split(values):
    high = values.astype(BF16)
    low = (values - high.astype(F32)).astype(BF16)
    return jnp.concatenate([high, low], axis=1)


def quotient(x, d):
    return lax.shift_right_logical(x, d.bit_length() - 1) if d & (d - 1) == 0 else x // d


def place(n):
    i, j = lax.axis_index("tx"), lax.axis_index("ty")
    return i, j, lax.rem(i, 2) == 0


def owners(n):
    i, j, even = place(n)
    mine = i * 2 + j
    return mine, jnp.where(even, mine + 2, mine - 2), jnp.where(even, mine - 2, mine + 2), mine + 1 - 2 * j


def spread(cols, lane, rows):
    return jnp.broadcast_to(cols[:, lane : lane + 1], (rows, 128)).astype(BF16)


def one_hot(where, first, count):
    parts = []
    for at in range(first, first + count, 128):
        lanes = (lax.broadcasted_iota(I32, where.shape, 1) + at).astype(F32).astype(BF16)
        parts.append(jnp.where(where == lanes, jnp.ones((), BF16), jnp.zeros((), BF16)))
    return jnp.concatenate(parts, axis=1)


def boundary_kernel(tiles, boundary):
    boundary[...] = tiles[: boundary.shape[0], :]


def local_kernel(
    n, co_rows, tiles, around_s, sources, parents, weights, edge_in, edge_bias, cols, near, scale, pool, lift, picked
):
    nodes, width = tiles.shape
    degree = near.shape[0]
    rim = nodes // 4
    j = lax.axis_index("ty")
    index = sources[...]
    ids = parents[...]
    block_of = quotient(ids, co_rows)
    slot = ids - block_of * co_rows
    for at, owner in enumerate(owners(n)):
        slot = jnp.where(block_of == owner, slot + at * co_rows, slot)
    slot = slot.astype(F32)
    piece = quotient(index, rim)
    low = index & (rim - 1)
    nowhere = 2 * rim
    rows = [
        ((index & (2 * rim - 1)) - rim).astype(F32),
        jnp.where(piece == 7 - j, low, nowhere).astype(F32),
        jnp.where((piece == 4) | (piece == 5), index - 5 * rim, nowhere).astype(F32),
        piece.astype(F32),
        slot,
        weights[...].astype(F32),
        jnp.zeros((6, nodes), F32),
    ]
    turned = jnp.concatenate(rows, axis=0).T
    cols[...] = turned
    scale[...] = turned[:, 4 * degree + 1 : 4 * degree + 2] * jnp.ones((1, width), F32)
    row = lax.broadcasted_iota(I32, pool.shape, 0).astype(F32).astype(BF16)
    pool[...] = jnp.where(row == slot.astype(BF16), jnp.ones((), BF16), jnp.zeros((), BF16))
    lift[...] = one_hot(spread(cols[...], 4 * degree, nodes), 0, 4 * co_rows)
    project = edge_in[1]
    empty = jnp.zeros_like(project)
    project = jnp.concatenate(
        [jnp.concatenate([project, empty], axis=1), jnp.concatenate([empty, project], axis=1)], axis=0
    )
    table = jnp.concatenate([tiles[: 2 * rim, :], tiles[2 * rim :, :]], axis=1)
    side = around_s[...]

    def step(at, _):
        first = pl.multiple_of(at * BLOCK, BLOCK)
        here = pl.ds(first, BLOCK)
        col = cols[here, :]
        for k in range(0, degree, GROUP):
            group = range(k, k + GROUP)
            ones = jnp.concatenate([one_hot(spread(col, g, BLOCK), -rim, 2 * rim) for g in group], axis=0)
            got = mm(ones, table).astype(BF16)
            ones = jnp.concatenate([one_hot(spread(col, degree + g, BLOCK), 0, rim) for g in group], axis=0)
            beside = mm(ones, side).astype(BF16)
            for g in group:
                part = slice((g - k) * BLOCK, (g - k + 1) * BLOCK)
                of = spread(col, 3 * degree + g, BLOCK)
                value = jnp.where(of < jnp.full((), 2, BF16), got[part, :width], got[part, width:])
                value = jnp.where(of < jnp.full((), 4, BF16), value, beside[part])
                picked[g // 2, here, g % 2 * width : (g % 2 + 1) * width] = value
        return 0

    lax.fori_loop(0, nodes // BLOCK, step, 0, unroll=UNROLL)
    dst = mm(tiles[...], edge_in[0]) + edge_bias[...]
    for pair in range(degree // 2):
        src = mm(picked[pair], project)
        near[2 * pair] = dst + src[:, :width]
        near[2 * pair + 1] = dst + src[:, width:]


def node_kernel(
    n, tiles, around_a, around_b, cols, near, scale, pool, edge_in, edge_out, node_in, node_bias, node_out, node_gain,
    fine_mid, own, to_a, to_b, to_s, total, weighted,
):
    nodes, width = tiles.shape
    degree = near.shape[0]
    rim = nodes // 4
    co_rows = own.shape[0]
    i, j, even = place(n)
    none = jnp.zeros(around_a.shape, BF16)
    got_a, got_b = around_a[...], around_b[...]
    before = jnp.where(i > 0, jnp.where(even, got_b, got_a), none)
    after = jnp.where(i < n - 1, jnp.where(even, got_a, got_b), none)
    table = split(mm(jnp.concatenate([before, after], axis=0), edge_in[1]))

    def step(at, _):
        first = pl.multiple_of(at * BLOCK, BLOCK)
        here = pl.ds(first, BLOCK)
        col = cols[here, :]
        sums = jnp.zeros((BLOCK, width), F32)
        for k in range(0, degree, GROUP):
            ones = [one_hot(spread(col, 2 * degree + k + g, BLOCK), -rim, 2 * rim) for g in range(GROUP)]
            got = mm(jnp.concatenate(ones, axis=0), table)
            for g in range(GROUP):
                part = got[g * BLOCK : (g + 1) * BLOCK]
                edge = near[k + g, here, :] + (part[:, :width] + part[:, width:])
                sums = sums + silu(edge).astype(BF16).astype(F32)
        total[here, :] = sums
        return 0

    lax.fori_loop(0, nodes // BLOCK, step, 0, unroll=UNROLL)
    node_weights = jnp.concatenate([node_in[0], node_in[1]], axis=0)
    out_twice = jnp.concatenate([edge_out[...], edge_out[...]], axis=0)
    for first in range(0, nodes, CHUNK):
        here = pl.ds(first, CHUNK)
        aggregate = mm(split(total[here, :]), out_twice).astype(BF16)
        both = jnp.concatenate([tiles[here, :], aggregate], axis=1)
        hidden = silu(mm(both, node_weights) + node_bias[...]).astype(BF16)
        update = normalise(mm(hidden, node_out[...]), node_gain[...])
        mid = (tiles[here, :].astype(F32) + update).astype(BF16)
        fine_mid[here, :] = mid
        weighted[here, :] = (mid.astype(F32) * scale[here, :]).astype(BF16)
    pooled = mm(pool[...], weighted[...])
    for at, ref in enumerate((own, to_a, to_b, to_s)):
        ref[...] = pooled[at * co_rows : (at + 1) * co_rows]


def base_kernel(fine_mid, prolong_in, base):
    base[...] = mm(fine_mid[...], prolong_in[0])


def coarse_kernel(state, own, from_a, from_b, from_s, coarse_gain, coarse_w, out):
    total = state[...].astype(F32) + own[...] + from_a[...] + from_b[...] + from_s[...]
    normed = normalise(total, coarse_gain[...]).astype(BF16)
    hidden = silu(mm(normed, coarse_w[0])).astype(BF16)
    out[...] = (total + mm(hidden, coarse_w[1])).astype(BF16)


def prolong_kernel(
    fine_mid, base, lift, own, from_a, from_b, from_s, prolong_in, prolong_out, out, coarse_out, ready, sems
):
    nodes, width = fine_mid.shape
    copies = [pltpu.make_async_copy(own, coarse_out, sems.at[PARTS])]
    copies[0].start()
    coarse = jnp.concatenate([own[...], from_a[...], from_b[...], from_s[...]], axis=0)
    terms = split(mm(coarse, prolong_in[1]))
    lifted = mm(lift[...], terms)
    hidden = silu(base[...] + (lifted[:, :width] + lifted[:, width:])).astype(BF16)
    block = nodes // PARTS
    for at in range(PARTS):
        part = slice(at * block, (at + 1) * block)
        here = pl.ds(at * block, block)
        ready[here, :] = (fine_mid[here, :].astype(F32) + mm(hidden[part], prolong_out[...])).astype(BF16)
        copies.append(pltpu.make_async_copy(ready.at[here], out.at[here], sems.at[at]))
        copies[-1].start()
    for copy in copies:
        copy.wait()


def call(kernel, outs, *args, flops=0, scratch=(), to=pltpu.VMEM):
    return pl.pallas_call(
        kernel,
        out_shape=outs,
        in_specs=[pl.BlockSpec(memory_space=pltpu.VMEM)] * len(args),
        out_specs=[pl.BlockSpec(memory_space=to)] * len(outs),
        scratch_shapes=scratch,
        compiler_params=pltpu.CompilerParams(vmem_limit_bytes=VMEM_LIMIT),
        cost_estimate=pl.CostEstimate(flops=flops, bytes_accessed=flops // 1000, transcendentals=0),
    )(*args)


def exchange(n, to_a, to_b, to_s):
    pairs_a = [(i, i ^ 1) for i in range(n)]
    pairs_b = []
    for i in range(n):
        for j in range(2):
            other = (((i - 1) ^ 1) + 1, j) if 0 < i < n - 1 else (i, 1 - j)
            pairs_b.append((i * 2 + j, other[0] * 2 + other[1]))
    return (
        lax.ppermute(to_a, "tx", pairs_a),
        lax.ppermute(to_b, ("tx", "ty"), pairs_b),
        lax.ppermute(to_s, "ty", [(0, 1), (1, 0)]),
    )


def body(
    tiles,
    sources,
    parents,
    restrict_w,
    coarse_state,
    edge_in,
    edge_bias,
    edge_out,
    node_in,
    node_bias,
    node_out,
    node_gain,
    coarse_gain,
    coarse_w,
    prolong_in,
    prolong_out,
):
    nodes, width = tiles.shape[2:]
    n = lax.axis_size("tx")
    co_rows = coarse_state.shape[0]
    degree = sources.shape[3]
    shape = jax.ShapeDtypeStruct

    latents = tiles[0, 0]
    (boundary,) = call(boundary_kernel, [shape((nodes // 4, width), BF16)], latents, flops=2**33)
    around_a, around_b, around_s = exchange(n, boundary, boundary, boundary)
    cols, near, scale, pool, lift = call(
        functools.partial(local_kernel, n, co_rows),
        [
            shape((nodes, 40), F32),
            shape((degree, nodes, width), F32),
            shape((nodes, width), F32),
            shape((4 * co_rows, nodes), BF16),
            shape((nodes, 4 * co_rows), BF16),
        ],
        latents, around_s, jnp.swapaxes(sources[0, 0], 0, 1), parents[0], restrict_w[0], edge_in, edge_bias[None],
        flops=2**34,
        scratch=[pltpu.VMEM((degree // 2, nodes, 2 * width), BF16)],
    )
    fine_mid, own, to_a, to_b, to_s = call(
        functools.partial(node_kernel, n),
        [shape((nodes, width), BF16)] + [shape((co_rows, width), F32)] * 4,
        latents, around_a, around_b, cols, near, scale, pool,
        edge_in, edge_out, node_in, node_bias[None], node_out, node_gain[None],
        flops=2**34,
        scratch=[pltpu.VMEM((nodes, width), F32), pltpu.VMEM((nodes, width), BF16)],
    )
    got = exchange(n, to_a, to_b, to_s)
    (coarse_out,) = call(
        coarse_kernel,
        [shape((co_rows, width), BF16)],
        coarse_state, own, *got, coarse_gain[None], coarse_w,
        flops=2**32,
    )
    beside = exchange(n, coarse_out, coarse_out, coarse_out)
    (base,) = call(base_kernel, [shape((nodes, width), F32)], fine_mid, prolong_in, flops=2**29)
    fine_out, coarse_out = call(
        prolong_kernel,
        [shape((nodes, width), BF16), shape((co_rows, width), BF16)],
        fine_mid, base, lift, coarse_out, *beside, prolong_in, prolong_out,
        to=pl.ANY,
        scratch=[pltpu.VMEM((nodes, width), BF16), pltpu.SemaphoreType.DMA((PARTS + 1,))],
        flops=2**32,
    )
    return (fine_out[None, None], coarse_out)


def solution(mesh):
    tile = P(("cases", "tx"), "ty", None, None)
    row = P(("cases", "tx"), "ty", None)
    coarse = P(("cases", "tx", "ty"), None)
    return jax.shard_map(
        body,
        mesh=mesh,
        in_specs=(tile, tile, row, row, coarse) + (P(),) * 11,
        out_specs=(tile, coarse),
        check_vma=False,
    )
```

```python
import functools

import jax
import jax.numpy as jnp
from jax import lax
from jax.experimental import pallas as pl
from jax.experimental.pallas import tpu as pltpu
from jax.sharding import PartitionSpec as P

F32 = jnp.float32
BF16 = jnp.bfloat16
I32 = jnp.int32
SENT = F32
VMEM_LIMIT = 32 * 1024 * 1024
BLOCK = 128
GROUP = 2
UNROLL = 8
CHUNK = 1024
PARTS = 4


def mm(a, b):
    return jnp.dot(a, b, preferred_element_type=F32)


def silu_of_twice(half):
    return half + half * jnp.tanh(half)


def normalise(values, gain):
    center = values - jnp.mean(values, axis=-1, keepdims=True)
    spread = jnp.mean(center * center, axis=-1, keepdims=True)
    return center * lax.rsqrt(spread + 1e-05) * gain


def split(values):
    high = values.astype(BF16)
    low = (values - high.astype(F32)).astype(BF16)
    return jnp.concatenate([high, low], axis=1)


def quotient(x, d):
    return lax.shift_right_logical(x, d.bit_length() - 1) if d & (d - 1) == 0 else x // d


def place(n):
    i, j = lax.axis_index("tx"), lax.axis_index("ty")
    return i, j, lax.rem(i, 2) == 0


def owners(n):
    i, j, even = place(n)
    mine = i * 2 + j
    return mine, jnp.where(even, mine + 2, mine - 2), jnp.where(even, mine - 2, mine + 2), mine + 1 - 2 * j


def spread(cols, lane, rows):
    return jnp.broadcast_to(cols[:, lane : lane + 1], (rows, 128)).astype(BF16)


def one_hot(where, first, count):
    parts = []
    for at in range(first, first + count, 128):
        lanes = (lax.broadcasted_iota(I32, where.shape, 1) + at).astype(F32).astype(BF16)
        parts.append(jnp.where(where == lanes, jnp.ones((), BF16), jnp.zeros((), BF16)))
    return jnp.concatenate(parts, axis=1)


def boundary_kernel(tiles, boundary):
    boundary[...] = tiles[: boundary.shape[0], :]


def local_kernel(n, co_rows, tiles, sources, parents, weights, cols, near, scale, pool, lift):
    nodes, width = tiles.shape
    degree = near.shape[0]
    rim = nodes // 4
    i, j, even = place(n)
    index = sources[...]
    ids = parents[...]
    block_of = quotient(ids, co_rows)
    slot = ids - block_of * co_rows
    for at, owner in enumerate(owners(n)):
        slot = jnp.where(block_of == owner, slot + at * co_rows, slot)
    slot = slot.astype(F32)
    piece = quotient(index, rim)
    low = index & (rim - 1)
    nowhere = 2 * rim
    inner = (i > 0) & (i < n - 1)
    piece_a, piece_b = jnp.where(even, 5, 4), jnp.where(inner, jnp.where(even, 4, 5), -1)
    rows = [
        jnp.where(piece < 4, (index & (2 * rim - 1)) - rim, nowhere).astype(F32),
        jnp.where((piece == piece_a) | (piece == 7 - j), low, nowhere).astype(F32),
        jnp.where(piece == piece_b, low, nowhere).astype(F32),
        piece.astype(F32),
        slot,
        weights[...].astype(F32),
        jnp.zeros((6, nodes), F32),
    ]
    turned = jnp.concatenate(rows, axis=0).T
    cols[...] = turned
    scale[...] = turned[:, 4 * degree + 1 : 4 * degree + 2] * jnp.ones((1, width), F32)
    row = lax.broadcasted_iota(I32, pool.shape, 0).astype(F32).astype(BF16)
    pool[...] = jnp.where(row == slot.astype(BF16), jnp.ones((), BF16), jnp.zeros((), BF16))
    lift[...] = one_hot(spread(cols[...], 4 * degree, nodes), 0, 4 * co_rows)
    table = jnp.concatenate([tiles[: 2 * rim, :], tiles[2 * rim :, :]], axis=1)

    def step(at, _):
        first = pl.multiple_of(at * BLOCK, BLOCK)
        here = pl.ds(first, BLOCK)
        col = cols[here, :]
        for k in range(0, degree, GROUP):
            group = range(k, k + GROUP)
            ones = jnp.concatenate([one_hot(spread(col, g, BLOCK), -rim, 2 * rim) for g in group], axis=0)
            got = mm(ones, table).astype(BF16)
            for g in group:
                part = slice((g - k) * BLOCK, (g - k + 1) * BLOCK)
                of = spread(col, 3 * degree + g, BLOCK)
                near[g, here, :] = jnp.where(of < jnp.full((), 2, BF16), got[part, :width], got[part, width:])
        return 0

    lax.fori_loop(0, nodes // BLOCK, step, 0, unroll=UNROLL)


def side_kernel(tiles, around_a, around_s, cols, near, edge_in, edge_bias, edges, picked):
    nodes, width = tiles.shape
    degree = near.shape[0]
    rim = nodes // 4
    table = jnp.concatenate([around_a[...], around_s[...]], axis=1)

    def step(at, _):
        first = pl.multiple_of(at * BLOCK, BLOCK)
        here = pl.ds(first, BLOCK)
        col = cols[here, :]
        for k in range(0, degree, GROUP):
            group = range(k, k + GROUP)
            ones = jnp.concatenate([one_hot(spread(col, degree + g, BLOCK), 0, rim) for g in group], axis=0)
            got = mm(ones, table).astype(BF16)
            for g in group:
                part = slice((g - k) * BLOCK, (g - k + 1) * BLOCK)
                of = spread(col, 3 * degree + g, BLOCK)
                value = jnp.where(of < jnp.full((), 6, BF16), got[part, :width], got[part, width:])
                picked[g // 2, here, g % 2 * width : (g % 2 + 1) * width] = value + near[g, here, :]
        return 0

    lax.fori_loop(0, nodes // BLOCK, step, 0, unroll=UNROLL)
    project = 0.5 * edge_in[1]
    empty = jnp.zeros_like(project)
    project = jnp.concatenate(
        [jnp.concatenate([project, empty], axis=1), jnp.concatenate([empty, project], axis=1)], axis=0
    )
    dst = mm(tiles[...], 0.5 * edge_in[0]) + 0.5 * edge_bias[...]
    for pair in range(degree // 2):
        src = mm(picked[pair], project)
        edges[2 * pair] = dst + src[:, :width]
        edges[2 * pair + 1] = dst + src[:, width:]


def node_kernel(
    tiles, around_b, cols, near, scale, pool, edge_in, edge_out, node_in, node_bias, node_out, node_gain,
    fine_mid, own, to_a, to_b, to_s, total, weighted,
):
    nodes, width = tiles.shape
    degree = near.shape[0]
    rim = nodes // 4
    co_rows = own.shape[0]
    table = split(mm(around_b[...], 0.5 * edge_in[1]))

    def step(at, _):
        first = pl.multiple_of(at * BLOCK, BLOCK)
        here = pl.ds(first, BLOCK)
        col = cols[here, :]
        sums = jnp.zeros((BLOCK, width), F32)
        for k in range(0, degree, GROUP):
            ones = [one_hot(spread(col, 2 * degree + k + g, BLOCK), 0, rim) for g in range(GROUP)]
            got = mm(jnp.concatenate(ones, axis=0), table)
            for g in range(GROUP):
                part = got[g * BLOCK : (g + 1) * BLOCK]
                edge = near[k + g, here, :] + (part[:, :width] + part[:, width:])
                sums = sums + silu_of_twice(edge).astype(BF16).astype(F32)
        total[here, :] = sums
        return 0

    lax.fori_loop(0, nodes // BLOCK, step, 0, unroll=UNROLL)
    node_weights = 0.5 * jnp.concatenate([node_in[0], node_in[1]], axis=0)
    out_twice = jnp.concatenate([edge_out[...], edge_out[...]], axis=0)
    for first in range(0, nodes, CHUNK):
        here = pl.ds(first, CHUNK)
        aggregate = mm(split(total[here, :]), out_twice).astype(BF16)
        both = jnp.concatenate([tiles[here, :], aggregate], axis=1)
        hidden = silu_of_twice(mm(both, node_weights) + 0.5 * node_bias[...]).astype(BF16)
        update = normalise(mm(hidden, node_out[...]), node_gain[...])
        mid = (tiles[here, :].astype(F32) + update).astype(BF16)
        fine_mid[here, :] = mid
        weighted[here, :] = (mid.astype(F32) * scale[here, :]).astype(BF16)
    pooled = mm(pool[...], weighted[...])
    for at, ref in enumerate((own, to_a, to_b, to_s)):
        ref[...] = pooled[at * co_rows : (at + 1) * co_rows].astype(ref.dtype)


def base_kernel(fine_mid, prolong_in, base):
    base[...] = mm(fine_mid[...], 0.5 * prolong_in[0])


def coarse_kernel(state, own, from_b, from_a, from_s, coarse_gain, coarse_w, *outs):
    total = state[...].astype(F32) + own[...]
    for ref in (from_a, from_b, from_s):
        total = total + ref[...].astype(F32)
    normed = normalise(total, coarse_gain[...]).astype(BF16)
    hidden = silu_of_twice(mm(normed, 0.5 * coarse_w[0])).astype(BF16)
    total = (total + mm(hidden, coarse_w[1])).astype(BF16)
    for out in outs:
        out[...] = total


def prolong_kernel(
    fine_mid, base, lift, own, from_a, from_b, from_s, prolong_in, prolong_out, out, coarse_out, ready, sems
):
    nodes, width = fine_mid.shape
    copies = [pltpu.make_async_copy(own, coarse_out, sems.at[PARTS])]
    copies[0].start()
    coarse = jnp.concatenate([own[...], from_a[...], from_b[...], from_s[...]], axis=0)
    terms = split(mm(coarse, 0.5 * prolong_in[1]))
    lifted = mm(lift[...], terms)
    hidden = silu_of_twice(base[...] + (lifted[:, :width] + lifted[:, width:])).astype(BF16)
    block = nodes // PARTS
    for at in range(PARTS):
        part = slice(at * block, (at + 1) * block)
        here = pl.ds(at * block, block)
        ready[here, :] = (fine_mid[here, :].astype(F32) + mm(hidden[part], prolong_out[...])).astype(BF16)
        copies.append(pltpu.make_async_copy(ready.at[here], out.at[here], sems.at[at]))
        copies[-1].start()
    for copy in copies:
        copy.wait()


def call(kernel, outs, *args, flops=0, scratch=(), to=pltpu.VMEM):
    return pl.pallas_call(
        kernel,
        out_shape=outs,
        in_specs=[pl.BlockSpec(memory_space=pltpu.VMEM)] * len(args),
        out_specs=[pl.BlockSpec(memory_space=to)] * len(outs),
        scratch_shapes=scratch,
        compiler_params=pltpu.CompilerParams(vmem_limit_bytes=VMEM_LIMIT),
        cost_estimate=pl.CostEstimate(flops=flops, bytes_accessed=flops // 1000, transcendentals=0),
    )(*args)


def exchange(n, to_a, to_b, to_s):
    pairs_a = [(i, i ^ 1) for i in range(n)]
    pairs_b = []
    for i in range(n):
        for j in range(2):
            other = (((i - 1) ^ 1) + 1, j) if 0 < i < n - 1 else (i, 1 - j)
            pairs_b.append((i * 2 + j, other[0] * 2 + other[1]))
    return (
        lax.ppermute(to_a, "tx", pairs_a),
        lax.ppermute(to_b, ("tx", "ty"), pairs_b),
        lax.ppermute(to_s, "ty", [(0, 1), (1, 0)]),
    )


def body(
    tiles,
    sources,
    parents,
    restrict_w,
    coarse_state,
    edge_in,
    edge_bias,
    edge_out,
    node_in,
    node_bias,
    node_out,
    node_gain,
    coarse_gain,
    coarse_w,
    prolong_in,
    prolong_out,
):
    nodes, width = tiles.shape[2:]
    n = lax.axis_size("tx")
    co_rows = coarse_state.shape[0]
    degree = sources.shape[3]
    shape = jax.ShapeDtypeStruct

    latents = tiles[0, 0]
    (boundary,) = call(boundary_kernel, [shape((nodes // 4, width), BF16)], latents, flops=2**33)
    around_a, around_b, around_s = exchange(n, boundary, boundary, boundary)
    cols, near, scale, pool, lift = call(
        functools.partial(local_kernel, n, co_rows),
        [
            shape((nodes, 40), F32),
            shape((degree, nodes, width), BF16),
            shape((nodes, width), F32),
            shape((4 * co_rows, nodes), BF16),
            shape((nodes, 4 * co_rows), BF16),
        ],
        latents, jnp.swapaxes(sources[0, 0], 0, 1), parents[0], restrict_w[0],
        flops=2**33,
    )
    (edges,) = call(
        side_kernel,
        [shape((degree, nodes, width), F32)],
        latents, around_a, around_s, cols, near, edge_in, edge_bias[None],
        flops=2**33,
        scratch=[pltpu.VMEM((degree // 2, nodes, 2 * width), BF16)],
    )
    fine_mid, own, to_a, to_b, to_s = call(
        node_kernel,
        [shape((nodes, width), BF16), shape((co_rows, width), F32)] + [shape((co_rows, width), SENT)] * 3,
        latents, around_b, cols, edges, scale, pool, edge_in, edge_out, node_in, node_bias[None], node_out, node_gain[None],
        flops=2**33,
        scratch=[pltpu.VMEM((nodes, width), F32), pltpu.VMEM((nodes, width), BF16)],
    )
    got = exchange(n, to_a, to_b, to_s)
    coarse_out, *sent = call(
        coarse_kernel,
        [shape((co_rows, width), BF16)] * 4,
        coarse_state, own, got[1], got[0], got[2], coarse_gain[None], coarse_w,
        flops=2**32,
    )
    beside = exchange(n, *sent)
    (base,) = call(base_kernel, [shape((nodes, width), F32)], fine_mid, prolong_in, flops=2**29)
    fine_out, coarse_out = call(
        prolong_kernel,
        [shape((nodes, width), BF16), shape((co_rows, width), BF16)],
        fine_mid, base, lift, coarse_out, beside[0], beside[1], beside[2], prolong_in, prolong_out,
        to=pl.ANY,
        scratch=[pltpu.VMEM((nodes, width), BF16), pltpu.SemaphoreType.DMA((PARTS + 1,))],
        flops=2**32,
    )
    return (fine_out[None, None], coarse_out)


def solution(mesh):
    tile = P(("cases", "tx"), "ty", None, None)
    row = P(("cases", "tx"), "ty", None)
    coarse = P(("cases", "tx", "ty"), None)
    return jax.shard_map(
        body,
        mesh=mesh,
        in_specs=(tile, tile, row, row, coarse) + (P(),) * 11,
        out_specs=(tile, coarse),
        check_vma=False,
    )
```

```python
import functools

import jax
import jax.numpy as jnp
from jax import lax
from jax.experimental import pallas as pl
from jax.experimental.pallas import tpu as pltpu
from jax.sharding import PartitionSpec as P

F32 = jnp.float32
BF16 = jnp.bfloat16
I32 = jnp.int32
VMEM_LIMIT = 32 * 1024 * 1024
BLOCK = 128
GROUP = 2
UNROLL = 8
CHUNK = 1024
PARTS = 4


def mm(a, b):
    return jnp.dot(a, b, preferred_element_type=F32)


def silu_of_twice(half):
    return half + half * jnp.tanh(half)


def normalise(values, gain):
    center = values - jnp.mean(values, axis=-1, keepdims=True)
    spread = jnp.mean(center * center, axis=-1, keepdims=True)
    return center * lax.rsqrt(spread + 1e-05) * gain


def two_terms(values):
    high = values.astype(BF16)
    return high, (values - high.astype(F32)).astype(BF16)


def split(values):
    return jnp.concatenate(two_terms(values), axis=1)


def rows_of(ref, at, count):
    return ref[at * count : (at + 1) * count, :]


def quotient(x, d):
    return lax.shift_right_logical(x, d.bit_length() - 1) if d & (d - 1) == 0 else x // d


def place(n):
    i, j = lax.axis_index("tx"), lax.axis_index("ty")
    return i, j, lax.rem(i, 2) == 0


def owners(n):
    i, j, even = place(n)
    mine = i * 2 + j
    return mine, jnp.where(even, mine + 2, mine - 2), jnp.where(even, mine - 2, mine + 2), mine + 1 - 2 * j


def spread(cols, lane, rows):
    return jnp.broadcast_to(cols[:, lane : lane + 1], (rows, 128)).astype(BF16)


def one_hot(where, first, count):
    parts = []
    for at in range(first, first + count, 128):
        lanes = (lax.broadcasted_iota(I32, where.shape, 1) + at).astype(F32).astype(BF16)
        parts.append(jnp.where(where == lanes, jnp.ones((), BF16), jnp.zeros((), BF16)))
    return jnp.concatenate(parts, axis=1)


def boundary_kernel(tiles, boundary):
    boundary[...] = tiles[: boundary.shape[0], :]


def local_kernel(n, co_rows, tiles, sources, parents, weights, cols, near, scale, pool, lift):
    nodes, width = tiles.shape
    degree = near.shape[0]
    rim = nodes // 4
    i, j, even = place(n)
    index = sources[...]
    ids = parents[...]
    block_of = quotient(ids, co_rows)
    slot = ids - block_of * co_rows
    for at, owner in enumerate(owners(n)):
        slot = jnp.where(block_of == owner, slot + at * co_rows, slot)
    slot = slot.astype(F32)
    piece = quotient(index, rim)
    low = index & (rim - 1)
    nowhere = 2 * rim
    inner = (i > 0) & (i < n - 1)
    piece_a, piece_b = jnp.where(even, 5, 4), jnp.where(inner, jnp.where(even, 4, 5), -1)
    rows = [
        jnp.where(piece < 4, (index & (2 * rim - 1)) - rim, nowhere).astype(F32),
        jnp.where((piece == piece_a) | (piece == 7 - j), low, nowhere).astype(F32),
        jnp.where(piece == piece_b, low, nowhere).astype(F32),
        piece.astype(F32),
        slot,
        weights[...].astype(F32),
        jnp.zeros((6, nodes), F32),
    ]
    turned = jnp.concatenate(rows, axis=0).T
    cols[...] = turned
    scale[...] = turned[:, 4 * degree + 1 : 4 * degree + 2] * jnp.ones((1, width), F32)
    row = lax.broadcasted_iota(I32, pool.shape, 0).astype(F32).astype(BF16)
    pool[...] = jnp.where(row == slot.astype(BF16), jnp.ones((), BF16), jnp.zeros((), BF16))
    lift[...] = one_hot(spread(cols[...], 4 * degree, nodes), 0, 4 * co_rows)
    table = jnp.concatenate([tiles[: 2 * rim, :], tiles[2 * rim :, :]], axis=1)

    def step(at, _):
        first = pl.multiple_of(at * BLOCK, BLOCK)
        here = pl.ds(first, BLOCK)
        col = cols[here, :]
        for k in range(0, degree, GROUP):
            group = range(k, k + GROUP)
            ones = jnp.concatenate([one_hot(spread(col, g, BLOCK), -rim, 2 * rim) for g in group], axis=0)
            got = mm(ones, table).astype(BF16)
            for g in group:
                part = slice((g - k) * BLOCK, (g - k + 1) * BLOCK)
                of = spread(col, 3 * degree + g, BLOCK)
                near[g, here, :] = jnp.where(of < jnp.full((), 2, BF16), got[part, :width], got[part, width:])
        return 0

    lax.fori_loop(0, nodes // BLOCK, step, 0, unroll=UNROLL)


def side_kernel(tiles, around_a, around_s, cols, near, edge_in, edge_bias, edges, picked):
    nodes, width = tiles.shape
    degree = near.shape[0]
    rim = nodes // 4
    table = jnp.concatenate([around_a[...], around_s[...]], axis=1)

    def step(at, _):
        first = pl.multiple_of(at * BLOCK, BLOCK)
        here = pl.ds(first, BLOCK)
        col = cols[here, :]
        for k in range(0, degree, GROUP):
            group = range(k, k + GROUP)
            ones = jnp.concatenate([one_hot(spread(col, degree + g, BLOCK), 0, rim) for g in group], axis=0)
            got = mm(ones, table).astype(BF16)
            for g in group:
                part = slice((g - k) * BLOCK, (g - k + 1) * BLOCK)
                of = spread(col, 3 * degree + g, BLOCK)
                value = jnp.where(of < jnp.full((), 6, BF16), got[part, :width], got[part, width:])
                picked[g // 2, here, g % 2 * width : (g % 2 + 1) * width] = value + near[g, here, :]
        return 0

    lax.fori_loop(0, nodes // BLOCK, step, 0, unroll=UNROLL)
    project = 0.5 * edge_in[1]
    empty = jnp.zeros_like(project)
    project = jnp.concatenate(
        [jnp.concatenate([project, empty], axis=1), jnp.concatenate([empty, project], axis=1)], axis=0
    )
    dst = mm(tiles[...], 0.5 * edge_in[0]) + 0.5 * edge_bias[...]
    for pair in range(degree // 2):
        src = mm(picked[pair], project)
        edges[2 * pair] = dst + src[:, :width]
        edges[2 * pair + 1] = dst + src[:, width:]


def node_kernel(
    tiles, around_b, cols, near, scale, pool, edge_in, edge_out, node_in, node_bias, node_out, node_gain, state,
    fine_mid, own, sums_out, total, weighted,
):
    nodes, width = tiles.shape
    degree = near.shape[0]
    rim = nodes // 4
    co_rows = own.shape[0]
    table = split(mm(around_b[...], 0.5 * edge_in[1]))

    def step(at, _):
        first = pl.multiple_of(at * BLOCK, BLOCK)
        here = pl.ds(first, BLOCK)
        col = cols[here, :]
        sums = jnp.zeros((BLOCK, width), F32)
        for k in range(0, degree, GROUP):
            ones = [one_hot(spread(col, 2 * degree + k + g, BLOCK), 0, rim) for g in range(GROUP)]
            got = mm(jnp.concatenate(ones, axis=0), table)
            for g in range(GROUP):
                part = got[g * BLOCK : (g + 1) * BLOCK]
                edge = near[k + g, here, :] + (part[:, :width] + part[:, width:])
                sums = sums + silu_of_twice(edge).astype(BF16).astype(F32)
        total[here, :] = sums
        return 0

    lax.fori_loop(0, nodes // BLOCK, step, 0, unroll=UNROLL)
    node_weights = 0.5 * jnp.concatenate([node_in[0], node_in[1]], axis=0)
    out_twice = jnp.concatenate([edge_out[...], edge_out[...]], axis=0)
    for first in range(0, nodes, CHUNK):
        here = pl.ds(first, CHUNK)
        aggregate = mm(split(total[here, :]), out_twice).astype(BF16)
        both = jnp.concatenate([tiles[here, :], aggregate], axis=1)
        hidden = silu_of_twice(mm(both, node_weights) + 0.5 * node_bias[...]).astype(BF16)
        update = normalise(mm(hidden, node_out[...]), node_gain[...])
        mid = (tiles[here, :].astype(F32) + update).astype(BF16)
        fine_mid[here, :] = mid
        weighted[here, :] = (mid.astype(F32) * scale[here, :]).astype(BF16)
    pooled = mm(pool[...], weighted[...])
    mine = pooled[:co_rows] + state[...].astype(F32)
    own[...] = mine
    high, low = two_terms(mine)
    to_a, to_b, to_s = (pooled[at * co_rows : (at + 1) * co_rows].astype(BF16) for at in (1, 2, 3))
    sums_out[...] = jnp.concatenate([high, low, to_s, to_a, to_b], axis=0)


def base_kernel(fine_mid, prolong_in, base):
    base[...] = mm(fine_mid[...], 0.5 * prolong_in[0])


def first_is_a(n):
    i, _, even = place(n)
    return even == (lax.rem(i, 4) < 2)


def share_kernel(n, own, sums, mate, near, mate_near, to_a, to_b, to_first, to_second):
    count = own.shape[0]
    _, _, mine_s, mine_a, mine_b = (rows_of(sums, at, count) for at in range(5))
    high, low, mate_s, mate_a, mate_b = (rows_of(mate, at, count) for at in range(5))
    total = own[...] + mate_s.astype(F32)
    near[...] = total
    mate_near[...] = high.astype(F32) + low.astype(F32) + mine_s.astype(F32)
    to_a[...] = jnp.concatenate([*two_terms(total), mine_a, mate_a], axis=0)
    to_b[...] = jnp.concatenate([*two_terms(total), mine_b, mate_b], axis=0)
    first = first_is_a(n)
    to_first[...] = jnp.where(first, mine_a, mine_b)
    to_second[...] = jnp.where(first, mine_b, mine_a)


def prolong_kernel(
    n, fine_mid, base, lift, near, mate_near, sums, from_b, from_a, from_first, from_second, coarse_gain, coarse_w,
    prolong_in, prolong_out, out, coarse_out, ready, coarse_ready, sems,
):
    nodes, width = fine_mid.shape
    count = near.shape[0]
    i, _, _ = place(n)
    far_first = from_first[...].astype(F32)
    far_second = jnp.where((i > 1) & (i < n - 2), from_second[...].astype(F32), 0.0)
    first = first_is_a(n)
    high_a, low_a, to_me_a, to_mate_a = (rows_of(from_a, at, count).astype(F32) for at in range(4))
    high_b, low_b, to_me_b, to_mate_b = (rows_of(from_b, at, count).astype(F32) for at in range(4))
    total = jnp.concatenate(
        [
            near[...] + to_me_a + to_me_b,
            high_a + low_a + rows_of(sums, 3, count).astype(F32) + jnp.where(first, far_first, far_second),
            high_b + low_b + rows_of(sums, 4, count).astype(F32) + jnp.where(first, far_second, far_first),
            mate_near[...] + to_mate_a + to_mate_b,
        ],
        axis=0,
    )
    normed = normalise(total, coarse_gain[...]).astype(BF16)
    hidden = silu_of_twice(mm(normed, 0.5 * coarse_w[0])).astype(BF16)
    coarse = (total + mm(hidden, coarse_w[1])).astype(BF16)
    coarse_ready[...] = coarse[:count]
    copies = [pltpu.make_async_copy(coarse_ready, coarse_out, sems.at[PARTS])]
    copies[0].start()
    terms = split(mm(coarse, 0.5 * prolong_in[1]))
    lifted = mm(lift[...], terms)
    hidden = silu_of_twice(base[...] + (lifted[:, :width] + lifted[:, width:])).astype(BF16)
    block = nodes // PARTS
    for at in range(PARTS):
        part = slice(at * block, (at + 1) * block)
        here = pl.ds(at * block, block)
        ready[here, :] = (fine_mid[here, :].astype(F32) + mm(hidden[part], prolong_out[...])).astype(BF16)
        copies.append(pltpu.make_async_copy(ready.at[here], out.at[here], sems.at[at]))
        copies[-1].start()
    for copy in copies:
        copy.wait()


def call(kernel, outs, *args, flops=0, scratch=(), to=pltpu.VMEM):
    return pl.pallas_call(
        kernel,
        out_shape=outs,
        in_specs=[pl.BlockSpec(memory_space=pltpu.VMEM)] * len(args),
        out_specs=[pl.BlockSpec(memory_space=to)] * len(outs),
        scratch_shapes=scratch,
        compiler_params=pltpu.CompilerParams(vmem_limit_bytes=VMEM_LIMIT),
        cost_estimate=pl.CostEstimate(flops=flops, bytes_accessed=flops // 1000, transcendentals=0),
    )(*args)


def pairs(n):
    def both(partner):
        steps = []
        for i in range(n):
            for j in range(2):
                k = partner(i)
                steps.append((i * 2 + j, k * 2 + j if 0 <= k < n else i * 2 + 1 - j))
        return steps

    return both(lambda i: i ^ 1), both(lambda i: ((i - 1) ^ 1) + 1), both(lambda i: i ^ 2), both(lambda i: ((i - 2) ^ 2) + 2)


def swap(value):
    return lax.ppermute(value, "ty", [(0, 1), (1, 0)])


def body(
    tiles,
    sources,
    parents,
    restrict_w,
    coarse_state,
    edge_in,
    edge_bias,
    edge_out,
    node_in,
    node_bias,
    node_out,
    node_gain,
    coarse_gain,
    coarse_w,
    prolong_in,
    prolong_out,
):
    nodes, width = tiles.shape[2:]
    n = lax.axis_size("tx")
    co_rows = coarse_state.shape[0]
    degree = sources.shape[3]
    shape = jax.ShapeDtypeStruct

    latents = tiles[0, 0]
    (boundary,) = call(boundary_kernel, [shape((nodes // 4, width), BF16)], latents, flops=2**33)
    pairs_a, pairs_b, pairs_first, pairs_second = pairs(n)
    all_tiles = ("tx", "ty")
    around_a = lax.ppermute(boundary, all_tiles, pairs_a)
    around_b = lax.ppermute(boundary, all_tiles, pairs_b)
    around_s = swap(boundary)
    cols, near, scale, pool, lift = call(
        functools.partial(local_kernel, n, co_rows),
        [
            shape((nodes, 40), F32),
            shape((degree, nodes, width), BF16),
            shape((nodes, width), F32),
            shape((4 * co_rows, nodes), BF16),
            shape((nodes, 4 * co_rows), BF16),
        ],
        latents, jnp.swapaxes(sources[0, 0], 0, 1), parents[0], restrict_w[0],
        flops=2**33,
    )
    (edges,) = call(
        side_kernel,
        [shape((degree, nodes, width), F32)],
        latents, around_a, around_s, cols, near, edge_in, edge_bias[None],
        flops=2**33,
        scratch=[pltpu.VMEM((degree // 2, nodes, 2 * width), BF16)],
    )
    fine_mid, own, sums = call(
        node_kernel,
        [shape((nodes, width), BF16), shape((co_rows, width), F32), shape((5 * co_rows, width), BF16)],
        latents, around_b, cols, edges, scale, pool, edge_in, edge_out, node_in, node_bias[None], node_out, node_gain[None],
        coarse_state,
        flops=2**33,
        scratch=[pltpu.VMEM((nodes, width), F32), pltpu.VMEM((nodes, width), BF16)],
    )
    near, mate_near, to_a, to_b, to_first, to_second = call(
        functools.partial(share_kernel, n),
        [shape((co_rows, width), F32)] * 2 + [shape((4 * co_rows, width), BF16)] * 2 + [shape((co_rows, width), BF16)] * 2,
        own, sums, swap(sums),
        flops=2**32,
    )
    (base,) = call(base_kernel, [shape((nodes, width), F32)], fine_mid, prolong_in, flops=2**29)
    fine_out, coarse_out = call(
        functools.partial(prolong_kernel, n),
        [shape((nodes, width), BF16), shape((co_rows, width), BF16)],
        fine_mid, base, lift, near, mate_near, sums,
        lax.ppermute(to_b, all_tiles, pairs_b),
        lax.ppermute(to_a, all_tiles, pairs_a),
        lax.ppermute(to_first, all_tiles, pairs_first),
        lax.ppermute(to_second, all_tiles, pairs_second),
        coarse_gain[None], coarse_w, prolong_in, prolong_out,
        to=pl.ANY,
        scratch=[
            pltpu.VMEM((nodes, width), BF16),
            pltpu.VMEM((co_rows, width), BF16),
            pltpu.SemaphoreType.DMA((PARTS + 1,)),
        ],
        flops=2**32,
    )
    return (fine_out[None, None], coarse_out)


def solution(mesh):
    tile = P(("cases", "tx"), "ty", None, None)
    row = P(("cases", "tx"), "ty", None)
    coarse = P(("cases", "tx", "ty"), None)
    return jax.shard_map(
        body,
        mesh=mesh,
        in_specs=(tile, tile, row, row, coarse) + (P(),) * 11,
        out_specs=(tile, coarse),
        check_vma=False,
    )
```

```python
import functools

import jax
import jax.numpy as jnp
from jax import lax
from jax.experimental import pallas as pl
from jax.experimental.pallas import tpu as pltpu
from jax.sharding import PartitionSpec as P

F32 = jnp.float32
BF16 = jnp.bfloat16
I32 = jnp.int32
VMEM_LIMIT = 32 * 1024 * 1024
BLOCK = 128
GROUP = 2
UNROLL = 8
CHUNK = 1024
PARTS = 4


def mm(a, b):
    return jnp.dot(a, b, preferred_element_type=F32)


def silu_of_twice(half):
    return half + half * jnp.tanh(half)


def normalise(values, gain):
    center = values - jnp.mean(values, axis=-1, keepdims=True)
    spread = jnp.mean(center * center, axis=-1, keepdims=True)
    return center * lax.rsqrt(spread + 1e-05) * gain


def two_terms(values):
    high = values.astype(BF16)
    return high, (values - high.astype(F32)).astype(BF16)


def split(values):
    return jnp.concatenate(two_terms(values), axis=1)


def rows_of(ref, at, count):
    return ref[at * count : (at + 1) * count, :]


def quotient(x, d):
    return lax.shift_right_logical(x, d.bit_length() - 1) if d & (d - 1) == 0 else x // d


def place(n):
    i, j = lax.axis_index("tx"), lax.axis_index("ty")
    return i, j, lax.rem(i, 2) == 0


def owners(n):
    i, j, even = place(n)
    mine = i * 2 + j
    return mine, jnp.where(even, mine + 2, mine - 2), jnp.where(even, mine - 2, mine + 2), mine + 1 - 2 * j


def spread(cols, lane, rows):
    return jnp.broadcast_to(cols[:, lane : lane + 1], (rows, 128)).astype(BF16)


def one_hot(where, first, count):
    parts = []
    for at in range(first, first + count, 128):
        lanes = (lax.broadcasted_iota(I32, where.shape, 1) + at).astype(F32).astype(BF16)
        parts.append(jnp.where(where == lanes, jnp.ones((), BF16), jnp.zeros((), BF16)))
    return jnp.concatenate(parts, axis=1)


def boundary_kernel(tiles, boundary):
    boundary[...] = tiles[: boundary.shape[0], :]


def local_kernel(n, co_rows, tiles, sources, parents, weights, cols, near, pieces, scale, pool):
    nodes, width = tiles.shape
    degree = near.shape[0]
    rim = nodes // 4
    i, j, even = place(n)
    index = sources[...]
    ids = parents[...]
    block_of = quotient(ids, co_rows)
    slot = ids - block_of * co_rows
    for at, owner in enumerate(owners(n)):
        slot = jnp.where(block_of == owner, slot + at * co_rows, slot)
    slot = slot.astype(F32)
    piece = quotient(index, rim)
    low = index & (rim - 1)
    nowhere = 2 * rim
    inner = (i > 0) & (i < n - 1)
    piece_a, piece_b = jnp.where(even, 5, 4), jnp.where(inner, jnp.where(even, 4, 5), -1)
    rows = [
        jnp.where(piece < 4, (index & (2 * rim - 1)) - rim, nowhere).astype(F32),
        jnp.where((piece == piece_a) | (piece == 7 - j), low, nowhere).astype(F32),
        jnp.where(piece == piece_b, low, nowhere).astype(F32),
        piece.astype(F32),
        slot,
        weights[...].astype(F32),
        jnp.zeros((6, nodes), F32),
    ]
    turned = jnp.concatenate(rows, axis=0).T
    cols[...] = turned
    table = jnp.concatenate([tiles[: 2 * rim, :], tiles[2 * rim :, :]], axis=1)

    def step(at, _):
        first = pl.multiple_of(at * BLOCK, BLOCK)
        here = pl.ds(first, BLOCK)
        col = cols[here, :]
        for k in range(0, degree, GROUP):
            group = range(k, k + GROUP)
            ones = jnp.concatenate([one_hot(spread(col, g, BLOCK), -rim, 2 * rim) for g in group], axis=0)
            got = mm(ones, table).astype(BF16)
            for g in group:
                part = slice((g - k) * BLOCK, (g - k + 1) * BLOCK)
                of = spread(col, 3 * degree + g, BLOCK)
                pieces[g, here, :] = of
                near[g, here, :] = jnp.where(of < jnp.full((), 2, BF16), got[part, :width], got[part, width:])
        return 0

    lax.fori_loop(0, nodes // BLOCK, step, 0, unroll=UNROLL)
    scale[...] = turned[:, 4 * degree + 1 : 4 * degree + 2] * jnp.ones((1, width), F32)
    row = lax.broadcasted_iota(I32, pool.shape, 0).astype(F32).astype(BF16)
    pool[...] = jnp.where(row == slot.astype(BF16), jnp.ones((), BF16), jnp.zeros((), BF16))


def side_kernel(tiles, around_a, around_s, cols, near, pieces, edge_in, edge_bias, edges, picked):
    nodes, width = tiles.shape
    degree = near.shape[0]
    rim = nodes // 4
    table = jnp.concatenate([around_a[...], around_s[...]], axis=1)

    def step(at, _):
        first = pl.multiple_of(at * BLOCK, BLOCK)
        here = pl.ds(first, BLOCK)
        col = cols[here, :]
        for k in range(0, degree, GROUP):
            group = range(k, k + GROUP)
            ones = jnp.concatenate([one_hot(spread(col, degree + g, BLOCK), 0, rim) for g in group], axis=0)
            got = mm(ones, table).astype(BF16)
            for g in group:
                part = slice((g - k) * BLOCK, (g - k + 1) * BLOCK)
                of = pieces[g, here, :]
                value = jnp.where(of < jnp.full((), 6, BF16), got[part, :width], got[part, width:])
                picked[g // 2, here, g % 2 * width : (g % 2 + 1) * width] = value + near[g, here, :]
        return 0

    lax.fori_loop(0, nodes // BLOCK, step, 0, unroll=UNROLL)
    project = 0.5 * edge_in[1]
    empty = jnp.zeros_like(project)
    project = jnp.concatenate(
        [jnp.concatenate([project, empty], axis=1), jnp.concatenate([empty, project], axis=1)], axis=0
    )
    dst = mm(tiles[...], 0.5 * edge_in[0]) + 0.5 * edge_bias[...]
    for pair in range(degree // 2):
        src = mm(picked[pair], project)
        edges[2 * pair] = dst + src[:, :width]
        edges[2 * pair + 1] = dst + src[:, width:]


def node_kernel(
    tiles, around_b, cols, near, scale, pool, edge_in, edge_out, node_in, node_bias, node_out, node_gain, state,
    fine_mid, own, sums_out, total, weighted,
):
    nodes, width = tiles.shape
    degree = near.shape[0]
    rim = nodes // 4
    co_rows = own.shape[0]
    table = split(mm(around_b[...], 0.5 * edge_in[1]))

    def step(at, _):
        first = pl.multiple_of(at * BLOCK, BLOCK)
        here = pl.ds(first, BLOCK)
        col = cols[here, :]
        sums = jnp.zeros((BLOCK, width), F32)
        for k in range(0, degree, GROUP):
            ones = [one_hot(spread(col, 2 * degree + k + g, BLOCK), 0, rim) for g in range(GROUP)]
            got = mm(jnp.concatenate(ones, axis=0), table)
            for g in range(GROUP):
                part = got[g * BLOCK : (g + 1) * BLOCK]
                edge = near[k + g, here, :] + (part[:, :width] + part[:, width:])
                sums = sums + silu_of_twice(edge).astype(BF16).astype(F32)
        total[here, :] = sums
        return 0

    lax.fori_loop(0, nodes // BLOCK, step, 0, unroll=UNROLL)
    node_weights = 0.5 * jnp.concatenate([node_in[0], node_in[1]], axis=0)
    out_twice = jnp.concatenate([edge_out[...], edge_out[...]], axis=0)
    out_f = node_out[...].astype(F32)
    centred = split(out_f - jnp.mean(out_f, axis=-1, keepdims=True))
    for first in range(0, nodes, CHUNK):
        here = pl.ds(first, CHUNK)
        aggregate = mm(split(total[here, :]), out_twice).astype(BF16)
        both = jnp.concatenate([tiles[here, :], aggregate], axis=1)
        hidden = silu_of_twice(mm(both, node_weights) + 0.5 * node_bias[...]).astype(BF16)
        center = mm(hidden, centred)
        center = center[:, :width] + center[:, width:]
        spread_of = jnp.mean(center * center, axis=-1, keepdims=True)
        update = center * lax.rsqrt(spread_of + 1e-05) * node_gain[...]
        mid = (tiles[here, :].astype(F32) + update).astype(BF16)
        fine_mid[here, :] = mid
        weighted[here, :] = (mid.astype(F32) * scale[here, :]).astype(BF16)
    pooled = mm(pool[...], weighted[...])
    mine = pooled[:co_rows] + state[...].astype(F32)
    own[...] = mine
    high, low = two_terms(mine)
    to_a, to_b, to_s = (pooled[at * co_rows : (at + 1) * co_rows].astype(BF16) for at in (1, 2, 3))
    sums_out[...] = jnp.concatenate([high, low, to_s, to_a, to_b], axis=0)


def base_kernel(fine_mid, cols, prolong_in, base, lift):
    lift[...] = one_hot(spread(cols[...], cols.shape[1] - 8, fine_mid.shape[0]), 0, lift.shape[1])
    base[...] = mm(fine_mid[...], 0.5 * prolong_in[0])


def first_is_a(n):
    i, _, even = place(n)
    return even == (lax.rem(i, 4) < 2)


def share_kernel(n, own, sums, mate, near, mate_near, to_a, to_b, to_first, to_second):
    count = own.shape[0]
    _, _, mine_s, mine_a, mine_b = (rows_of(sums, at, count) for at in range(5))
    high, low, mate_s, mate_a, mate_b = (rows_of(mate, at, count) for at in range(5))
    total = own[...] + mate_s.astype(F32)
    near[...] = total
    mate_near[...] = high.astype(F32) + low.astype(F32) + mine_s.astype(F32)
    to_a[...] = jnp.concatenate([*two_terms(total), mine_a, mate_a], axis=0)
    to_b[...] = jnp.concatenate([*two_terms(total), mine_b, mate_b], axis=0)
    first = first_is_a(n)
    to_first[...] = jnp.where(first, mine_a, mine_b)
    to_second[...] = jnp.where(first, mine_b, mine_a)


def prolong_kernel(
    n, fine_mid, base, lift, near, mate_near, sums, from_b, from_a, from_first, from_second, coarse_gain, coarse_w,
    prolong_in, prolong_out, out, coarse_out, ready, coarse_ready, sems,
):
    nodes, width = fine_mid.shape
    count = near.shape[0]
    i, _, _ = place(n)
    far_first = from_first[...].astype(F32)
    far_second = jnp.where((i > 1) & (i < n - 2), from_second[...].astype(F32), 0.0)
    first = first_is_a(n)
    high_a, low_a, to_me_a, to_mate_a = (rows_of(from_a, at, count).astype(F32) for at in range(4))
    high_b, low_b, to_me_b, to_mate_b = (rows_of(from_b, at, count).astype(F32) for at in range(4))
    total = jnp.concatenate(
        [
            near[...] + to_me_a + to_me_b,
            high_a + low_a + rows_of(sums, 3, count).astype(F32) + jnp.where(first, far_first, far_second),
            high_b + low_b + rows_of(sums, 4, count).astype(F32) + jnp.where(first, far_second, far_first),
            mate_near[...] + to_mate_a + to_mate_b,
        ],
        axis=0,
    )
    normed = normalise(total, coarse_gain[...]).astype(BF16)
    hidden = silu_of_twice(mm(normed, 0.5 * coarse_w[0])).astype(BF16)
    coarse = (total + mm(hidden, coarse_w[1])).astype(BF16)
    coarse_ready[...] = coarse[:count]
    copies = [pltpu.make_async_copy(coarse_ready, coarse_out, sems.at[PARTS])]
    copies[0].start()
    terms = split(mm(coarse, 0.5 * prolong_in[1]))
    lifted = mm(lift[...], terms)
    hidden = silu_of_twice(base[...] + (lifted[:, :width] + lifted[:, width:])).astype(BF16)
    block = nodes // PARTS
    for at in range(PARTS):
        part = slice(at * block, (at + 1) * block)
        here = pl.ds(at * block, block)
        ready[here, :] = (fine_mid[here, :].astype(F32) + mm(hidden[part], prolong_out[...])).astype(BF16)
        copies.append(pltpu.make_async_copy(ready.at[here], out.at[here], sems.at[at]))
        copies[-1].start()
    for copy in copies:
        copy.wait()


def call(kernel, outs, *args, flops=0, scratch=(), to=pltpu.VMEM):
    return pl.pallas_call(
        kernel,
        out_shape=outs,
        in_specs=[pl.BlockSpec(memory_space=pltpu.VMEM)] * len(args),
        out_specs=[pl.BlockSpec(memory_space=to)] * len(outs),
        scratch_shapes=scratch,
        compiler_params=pltpu.CompilerParams(vmem_limit_bytes=VMEM_LIMIT),
        cost_estimate=pl.CostEstimate(flops=flops, bytes_accessed=flops // 1000, transcendentals=0),
    )(*args)


def pairs(n):
    def both(partner):
        steps = []
        for i in range(n):
            for j in range(2):
                k = partner(i)
                steps.append((i * 2 + j, k * 2 + j if 0 <= k < n else i * 2 + 1 - j))
        return steps

    return both(lambda i: i ^ 1), both(lambda i: ((i - 1) ^ 1) + 1), both(lambda i: i ^ 2), both(lambda i: ((i - 2) ^ 2) + 2)


def swap(value):
    return lax.ppermute(value, "ty", [(0, 1), (1, 0)])


def body(
    tiles,
    sources,
    parents,
    restrict_w,
    coarse_state,
    edge_in,
    edge_bias,
    edge_out,
    node_in,
    node_bias,
    node_out,
    node_gain,
    coarse_gain,
    coarse_w,
    prolong_in,
    prolong_out,
):
    nodes, width = tiles.shape[2:]
    n = lax.axis_size("tx")
    co_rows = coarse_state.shape[0]
    degree = sources.shape[3]
    shape = jax.ShapeDtypeStruct

    latents = tiles[0, 0]
    (boundary,) = call(boundary_kernel, [shape((nodes // 4, width), BF16)], latents, flops=2**33)
    pairs_a, pairs_b, pairs_first, pairs_second = pairs(n)
    all_tiles = ("tx", "ty")
    around_a = lax.ppermute(boundary, all_tiles, pairs_a)
    around_b = lax.ppermute(boundary, all_tiles, pairs_b)
    around_s = swap(boundary)
    cols, near, pieces, scale, pool = call(
        functools.partial(local_kernel, n, co_rows),
        [
            shape((nodes, 40), F32),
            shape((degree, nodes, width), BF16),
            shape((degree, nodes, width), BF16),
            shape((nodes, width), F32),
            shape((4 * co_rows, nodes), BF16),
        ],
        latents, jnp.swapaxes(sources[0, 0], 0, 1), parents[0], restrict_w[0],
        flops=2**33,
    )
    (edges,) = call(
        side_kernel,
        [shape((degree, nodes, width), F32)],
        latents, around_a, around_s, cols, near, pieces, edge_in, edge_bias[None],
        flops=2**33,
        scratch=[pltpu.VMEM((degree // 2, nodes, 2 * width), BF16)],
    )
    fine_mid, own, sums = call(
        node_kernel,
        [shape((nodes, width), BF16), shape((co_rows, width), F32), shape((5 * co_rows, width), BF16)],
        latents, around_b, cols, edges, scale, pool, edge_in, edge_out, node_in, node_bias[None], node_out, node_gain[None],
        coarse_state,
        flops=2**33,
        scratch=[pltpu.VMEM((nodes, width), F32), pltpu.VMEM((nodes, width), BF16)],
    )
    near, mate_near, to_a, to_b, to_first, to_second = call(
        functools.partial(share_kernel, n),
        [shape((co_rows, width), F32)] * 2 + [shape((4 * co_rows, width), BF16)] * 2 + [shape((co_rows, width), BF16)] * 2,
        own, sums, swap(sums),
        flops=2**32,
    )
    base, lift = call(
        base_kernel,
        [shape((nodes, width), F32), shape((nodes, 4 * co_rows), BF16)],
        fine_mid, cols, prolong_in,
        flops=2**29,
    )
    fine_out, coarse_out = call(
        functools.partial(prolong_kernel, n),
        [shape((nodes, width), BF16), shape((co_rows, width), BF16)],
        fine_mid, base, lift, near, mate_near, sums,
        lax.ppermute(to_b, all_tiles, pairs_b),
        lax.ppermute(to_a, all_tiles, pairs_a),
        lax.ppermute(to_first, all_tiles, pairs_first),
        lax.ppermute(to_second, all_tiles, pairs_second),
        coarse_gain[None], coarse_w, prolong_in, prolong_out,
        to=pl.ANY,
        scratch=[
            pltpu.VMEM((nodes, width), BF16),
            pltpu.VMEM((co_rows, width), BF16),
            pltpu.SemaphoreType.DMA((PARTS + 1,)),
        ],
        flops=2**32,
    )
    return (fine_out[None, None], coarse_out)


def solution(mesh):
    tile = P(("cases", "tx"), "ty", None, None)
    row = P(("cases", "tx"), "ty", None)
    coarse = P(("cases", "tx", "ty"), None)
    return jax.shard_map(
        body,
        mesh=mesh,
        in_specs=(tile, tile, row, row, coarse) + (P(),) * 11,
        out_specs=(tile, coarse),
        check_vma=False,
    )
```

```python
import functools

import jax
import jax.numpy as jnp
from jax import lax
from jax.experimental import pallas as pl
from jax.experimental.pallas import tpu as pltpu
from jax.sharding import PartitionSpec as P

F32 = jnp.float32
BF16 = jnp.bfloat16
I32 = jnp.int32
VMEM_LIMIT = 32 * 1024 * 1024
BLOCK = 128
GROUP = 2
UNROLL = 8
CHUNK = 1024
PARTS = 4


def mm(a, b):
    return jnp.dot(a, b, preferred_element_type=F32)


def silu_of_twice(half):
    return half + half * jnp.tanh(half)


def normalise(values, gain):
    center = values - jnp.mean(values, axis=-1, keepdims=True)
    spread = jnp.mean(center * center, axis=-1, keepdims=True)
    return center * lax.rsqrt(spread + 1e-05) * gain


def two_terms(values):
    high = values.astype(BF16)
    return high, (values - high.astype(F32)).astype(BF16)


def split(values):
    return jnp.concatenate(two_terms(values), axis=1)


def rows_of(ref, at, count):
    return ref[at * count : (at + 1) * count, :]


def quotient(x, d):
    return lax.shift_right_logical(x, d.bit_length() - 1) if d & (d - 1) == 0 else x // d


def place(n):
    i, j = lax.axis_index("tx"), lax.axis_index("ty")
    return i, j, lax.rem(i, 2) == 0


def owners(n):
    i, j, even = place(n)
    mine = i * 2 + j
    return mine, jnp.where(even, mine + 2, mine - 2), jnp.where(even, mine - 2, mine + 2), mine + 1 - 2 * j


def spread(cols, lane, rows):
    return jnp.broadcast_to(cols[:, lane : lane + 1], (rows, 128)).astype(BF16)


def one_hot(where, first, count):
    parts = []
    for at in range(first, first + count, 128):
        lanes = (lax.broadcasted_iota(I32, where.shape, 1) + at).astype(F32).astype(BF16)
        parts.append(jnp.where(where == lanes, jnp.ones((), BF16), jnp.zeros((), BF16)))
    return jnp.concatenate(parts, axis=1)


def boundary_kernel(tiles, boundary):
    boundary[...] = tiles[: boundary.shape[0], :]


def local_kernel(n, co_rows, tiles, sources, parents, weights, cols, near, pieces, scale, pool):
    nodes, width = tiles.shape
    degree = near.shape[0]
    rim = nodes // 4
    i, j, even = place(n)
    index = sources[...]
    ids = parents[...]
    block_of = quotient(ids, co_rows)
    slot = ids - block_of * co_rows
    for at, owner in enumerate(owners(n)):
        slot = jnp.where(block_of == owner, slot + at * co_rows, slot)
    slot = slot.astype(F32)
    piece = quotient(index, rim)
    low = index & (rim - 1)
    nowhere = 2 * rim
    inner = (i > 0) & (i < n - 1)
    piece_a, piece_b = jnp.where(even, 5, 4), jnp.where(inner, jnp.where(even, 4, 5), -1)
    rows = [
        jnp.where(piece < 4, (index & (2 * rim - 1)) - rim, nowhere).astype(F32),
        jnp.where((piece == piece_a) | (piece == piece_b) | (piece == 7 - j), low, nowhere).astype(F32),
        piece.astype(F32),
        slot,
        weights[...].astype(F32),
        jnp.zeros((6, nodes), F32),
    ]
    turned = jnp.concatenate(rows, axis=0).T
    cols[...] = turned
    table = jnp.concatenate([tiles[: 2 * rim, :], tiles[2 * rim :, :]], axis=1)

    def step(at, _):
        first = pl.multiple_of(at * BLOCK, BLOCK)
        here = pl.ds(first, BLOCK)
        col = cols[here, :]
        for k in range(0, degree, GROUP):
            group = range(k, k + GROUP)
            ones = jnp.concatenate([one_hot(spread(col, g, BLOCK), -rim, 2 * rim) for g in group], axis=0)
            got = mm(ones, table).astype(BF16)
            for g in group:
                part = slice((g - k) * BLOCK, (g - k + 1) * BLOCK)
                of = spread(col, 2 * degree + g, BLOCK)
                pieces[g, here, :] = of
                near[g, here, :] = jnp.where(of < jnp.full((), 2, BF16), got[part, :width], got[part, width:])
        return 0

    lax.fori_loop(0, nodes // BLOCK, step, 0, unroll=UNROLL)
    scale[...] = turned[:, 3 * degree + 1 : 3 * degree + 2] * jnp.ones((1, width), F32)
    row = lax.broadcasted_iota(I32, pool.shape, 0).astype(F32).astype(BF16)
    pool[...] = jnp.where(row == slot.astype(BF16), jnp.ones((), BF16), jnp.zeros((), BF16))


def node_kernel(
    n, tiles, around_s, around_a, around_b, cols, near, pieces, scale, pool,
    edge_in, edge_bias, edge_out, node_in, node_bias, node_out, node_gain, state,
    fine_mid, own, sums_out, total, weighted, picked,
):
    nodes, width = tiles.shape
    degree = near.shape[0]
    rim = nodes // 4
    co_rows = own.shape[0]
    _, _, even = place(n)
    got_a, got_b = around_a[...], around_b[...]
    table = jnp.concatenate([jnp.where(even, got_b, got_a), jnp.where(even, got_a, got_b), around_s[...]], axis=1)
    for at in range(nodes // BLOCK):
        here = slice(at * BLOCK, (at + 1) * BLOCK)
        col = cols[here, :]
        for k in range(0, degree, GROUP):
            group = range(k, k + GROUP)
            ones = jnp.concatenate([one_hot(spread(col, degree + g, BLOCK), 0, rim) for g in group], axis=0)
            got = mm(ones, table).astype(BF16)
            for g in group:
                part = got[(g - k) * BLOCK : (g - k + 1) * BLOCK]
                of = pieces[g, here, :]
                value = jnp.where(of < jnp.full((), 5, BF16), part[:, :width], part[:, width : 2 * width])
                value = jnp.where(of < jnp.full((), 6, BF16), value, part[:, 2 * width :])
                picked[g // 2, here, g % 2 * width : (g % 2 + 1) * width] = value + near[g, here, :]
    project = 0.5 * edge_in[1]
    empty = jnp.zeros_like(project)
    project = jnp.concatenate(
        [jnp.concatenate([project, empty], axis=1), jnp.concatenate([empty, project], axis=1)], axis=0
    )
    dst = mm(tiles[...], 0.5 * edge_in[0]) + 0.5 * edge_bias[...]
    sums = jnp.zeros((nodes, width), F32)
    for pair in range(degree // 2):
        src = mm(picked[pair], project)
        for part in (src[:, :width], src[:, width:]):
            sums = sums + silu_of_twice(dst + part).astype(BF16).astype(F32)
    total[...] = sums
    node_weights = 0.5 * jnp.concatenate([node_in[0], node_in[1]], axis=0)
    out_twice = jnp.concatenate([edge_out[...], edge_out[...]], axis=0)
    out_f = node_out[...].astype(F32)
    centred = split(out_f - jnp.mean(out_f, axis=-1, keepdims=True))
    for first in range(0, nodes, CHUNK):
        here = pl.ds(first, CHUNK)
        aggregate = mm(split(total[here, :]), out_twice).astype(BF16)
        both = jnp.concatenate([tiles[here, :], aggregate], axis=1)
        hidden = silu_of_twice(mm(both, node_weights) + 0.5 * node_bias[...]).astype(BF16)
        center = mm(hidden, centred)
        center = center[:, :width] + center[:, width:]
        spread_of = jnp.mean(center * center, axis=-1, keepdims=True)
        update = center * lax.rsqrt(spread_of + 1e-05) * node_gain[...]
        mid = (tiles[here, :].astype(F32) + update).astype(BF16)
        fine_mid[here, :] = mid
        weighted[here, :] = (mid.astype(F32) * scale[here, :]).astype(BF16)
    pooled = mm(pool[...], weighted[...])
    mine = pooled[:co_rows] + state[...].astype(F32)
    own[...] = mine
    high, low = two_terms(mine)
    to_a, to_b, to_s = (pooled[at * co_rows : (at + 1) * co_rows].astype(BF16) for at in (1, 2, 3))
    sums_out[...] = jnp.concatenate([high, low, to_s, to_a, to_b], axis=0)


def base_kernel(fine_mid, cols, prolong_in, base, lift):
    lift[...] = one_hot(spread(cols[...], cols.shape[1] - 8, fine_mid.shape[0]), 0, lift.shape[1])
    base[...] = mm(fine_mid[...], 0.5 * prolong_in[0])


def first_is_a(n):
    i, _, even = place(n)
    return even == (lax.rem(i, 4) < 2)


def share_kernel(n, own, sums, mate, near, mate_near, to_a, to_b, to_first, to_second):
    count = own.shape[0]
    _, _, mine_s, mine_a, mine_b = (rows_of(sums, at, count) for at in range(5))
    high, low, mate_s, mate_a, mate_b = (rows_of(mate, at, count) for at in range(5))
    total = own[...] + mate_s.astype(F32)
    near[...] = total
    mate_near[...] = high.astype(F32) + low.astype(F32) + mine_s.astype(F32)
    to_a[...] = jnp.concatenate([*two_terms(total), mine_a, mate_a], axis=0)
    to_b[...] = jnp.concatenate([*two_terms(total), mine_b, mate_b], axis=0)
    first = first_is_a(n)
    to_first[...] = jnp.where(first, mine_a, mine_b)
    to_second[...] = jnp.where(first, mine_b, mine_a)


def prolong_kernel(
    n, fine_mid, base, lift, near, mate_near, sums, from_a, from_first, from_b, from_second, coarse_gain, coarse_w,
    prolong_in, prolong_out, out, coarse_out, ready, coarse_ready, sems,
):
    nodes, width = fine_mid.shape
    count = near.shape[0]
    i, _, _ = place(n)
    far_first = from_first[...].astype(F32)
    far_second = jnp.where((i > 1) & (i < n - 2), from_second[...].astype(F32), 0.0)
    first = first_is_a(n)
    high_a, low_a, to_me_a, to_mate_a = (rows_of(from_a, at, count).astype(F32) for at in range(4))
    high_b, low_b, to_me_b, to_mate_b = (rows_of(from_b, at, count).astype(F32) for at in range(4))
    total = jnp.concatenate(
        [
            near[...] + to_me_a + to_me_b,
            high_a + low_a + rows_of(sums, 3, count).astype(F32) + jnp.where(first, far_first, far_second),
            high_b + low_b + rows_of(sums, 4, count).astype(F32) + jnp.where(first, far_second, far_first),
            mate_near[...] + to_mate_a + to_mate_b,
        ],
        axis=0,
    )
    normed = normalise(total, coarse_gain[...]).astype(BF16)
    hidden = silu_of_twice(mm(normed, 0.5 * coarse_w[0])).astype(BF16)
    coarse = (total + mm(hidden, coarse_w[1])).astype(BF16)
    coarse_ready[...] = coarse[:count]
    copies = [pltpu.make_async_copy(coarse_ready, coarse_out, sems.at[PARTS])]
    copies[0].start()
    terms = split(mm(coarse, 0.5 * prolong_in[1]))
    lifted = mm(lift[...], terms)
    hidden = silu_of_twice(base[...] + (lifted[:, :width] + lifted[:, width:])).astype(BF16)
    block = nodes // PARTS
    for at in range(PARTS):
        part = slice(at * block, (at + 1) * block)
        here = pl.ds(at * block, block)
        ready[here, :] = (fine_mid[here, :].astype(F32) + mm(hidden[part], prolong_out[...])).astype(BF16)
        copies.append(pltpu.make_async_copy(ready.at[here], out.at[here], sems.at[at]))
        copies[-1].start()
    for copy in copies:
        copy.wait()


def call(kernel, outs, *args, flops=0, scratch=(), to=pltpu.VMEM):
    return pl.pallas_call(
        kernel,
        out_shape=outs,
        in_specs=[pl.BlockSpec(memory_space=pltpu.VMEM)] * len(args),
        out_specs=[pl.BlockSpec(memory_space=to)] * len(outs),
        scratch_shapes=scratch,
        compiler_params=pltpu.CompilerParams(vmem_limit_bytes=VMEM_LIMIT),
        cost_estimate=pl.CostEstimate(flops=flops, bytes_accessed=flops // 1000, transcendentals=0),
    )(*args)


def pairs(n):
    def both(partner):
        steps = []
        for i in range(n):
            for j in range(2):
                k = partner(i)
                steps.append((i * 2 + j, k * 2 + j if 0 <= k < n else i * 2 + 1 - j))
        return steps

    return both(lambda i: i ^ 1), both(lambda i: ((i - 1) ^ 1) + 1), both(lambda i: i ^ 2), both(lambda i: ((i - 2) ^ 2) + 2)


def swap(value):
    return lax.ppermute(value, "ty", [(0, 1), (1, 0)])


def body(
    tiles,
    sources,
    parents,
    restrict_w,
    coarse_state,
    edge_in,
    edge_bias,
    edge_out,
    node_in,
    node_bias,
    node_out,
    node_gain,
    coarse_gain,
    coarse_w,
    prolong_in,
    prolong_out,
):
    nodes, width = tiles.shape[2:]
    n = lax.axis_size("tx")
    co_rows = coarse_state.shape[0]
    degree = sources.shape[3]
    shape = jax.ShapeDtypeStruct

    latents = tiles[0, 0]
    (boundary,) = call(boundary_kernel, [shape((nodes // 4, width), BF16)], latents, flops=2**33)
    pairs_a, pairs_b, pairs_first, pairs_second = pairs(n)
    all_tiles = ("tx", "ty")
    around_a = lax.ppermute(boundary, all_tiles, pairs_a)
    around_b = lax.ppermute(boundary, all_tiles, pairs_b)
    around_s = swap(boundary)
    cols, near, pieces, scale, pool = call(
        functools.partial(local_kernel, n, co_rows),
        [
            shape((nodes, 32), F32),
            shape((degree, nodes, width), BF16),
            shape((degree, nodes, width), BF16),
            shape((nodes, width), F32),
            shape((4 * co_rows, nodes), BF16),
        ],
        latents, jnp.swapaxes(sources[0, 0], 0, 1), parents[0], restrict_w[0],
        flops=2**33,
    )
    fine_mid, own, sums = call(
        functools.partial(node_kernel, n),
        [shape((nodes, width), BF16), shape((co_rows, width), F32), shape((5 * co_rows, width), BF16)],
        latents, around_s, around_a, around_b, cols, near, pieces, scale, pool,
        edge_in, edge_bias[None], edge_out, node_in, node_bias[None], node_out, node_gain[None], coarse_state,
        flops=2**33,
        scratch=[
            pltpu.VMEM((nodes, width), F32),
            pltpu.VMEM((nodes, width), BF16),
            pltpu.VMEM((degree // 2, nodes, 2 * width), BF16),
        ],
    )
    near, mate_near, to_a, to_b, to_first, to_second = call(
        functools.partial(share_kernel, n),
        [shape((co_rows, width), F32)] * 2 + [shape((4 * co_rows, width), BF16)] * 2 + [shape((co_rows, width), BF16)] * 2,
        own, sums, swap(sums),
        flops=2**32,
    )
    base, lift = call(
        base_kernel,
        [shape((nodes, width), F32), shape((nodes, 4 * co_rows), BF16)],
        fine_mid, cols, prolong_in,
        flops=2**29,
    )
    fine_out, coarse_out = call(
        functools.partial(prolong_kernel, n),
        [shape((nodes, width), BF16), shape((co_rows, width), BF16)],
        fine_mid, base, lift, near, mate_near, sums,
        lax.ppermute(to_a, all_tiles, pairs_a),
        lax.ppermute(to_first, all_tiles, pairs_first),
        lax.ppermute(to_b, all_tiles, pairs_b),
        lax.ppermute(to_second, all_tiles, pairs_second),
        coarse_gain[None], coarse_w, prolong_in, prolong_out,
        to=pl.ANY,
        scratch=[
            pltpu.VMEM((nodes, width), BF16),
            pltpu.VMEM((co_rows, width), BF16),
            pltpu.SemaphoreType.DMA((PARTS + 1,)),
        ],
        flops=2**32,
    )
    return (fine_out[None, None], coarse_out)


def solution(mesh):
    tile = P(("cases", "tx"), "ty", None, None)
    row = P(("cases", "tx"), "ty", None)
    coarse = P(("cases", "tx", "ty"), None)
    return jax.shard_map(
        body,
        mesh=mesh,
        in_specs=(tile, tile, row, row, coarse) + (P(),) * 11,
        out_specs=(tile, coarse),
        check_vma=False,
    )
```
